512 devices in a mesh: frames: 64 (over z, y_hi, core), coords: 8 (over y_lo, x).
Axes of the slice: x: 4, y: 8 (y_hi: 4, y_lo: 2; y = y_hi * 2 + y_lo), z: 8, core: 2. Of those that a mesh axis runs over, the one named last changes fastest.
Arguments:
- frames_xyz: bfloat16 [6144, 3, 65536], P('frames', None, 'coords'), may hold values from -120 to 120
- mean_xyz: float32 [3, 65536], P(None, 'coords'), may hold values from -60 to 60
- vector_block: bfloat16 [32, 3, 65536], P(None, None, ('coords', 'frames')), may hold values from -6 to 6
Outputs:
- product: float32 [32, 3, 65536], P(None, None, ('coords', 'frames'))
The draws below stay inside these ranges and needn't reach their ends.
All inputs are finite; a program needn't handle non-finite values.
Results may differ from the reference program's by a relative error of at most 0.0049.
Values may be sent and summed in bfloat16 or wider, within the bound.
No kernel may reach another device: no remote copies, remote signals or barrier semaphores. Data moves between devices by JAX's collectives and lax.ppermute only.
A program may use at most 64 MiB of HBM per device.

```python
import math
import jax
import jax.numpy as jnp
from jax import lax

NATOM = 65536
K = 32
NS_STEPS = 8
FRAMES = 6144


def mean_shape(key):
    ramp_top = 3.0
    offset = 1.0
    spots = jnp.arange(NATOM, dtype=jnp.float32) / NATOM
    ramp = jnp.exp(jnp.log(ramp_top) * spots)
    scales = jnp.array([3.0, 2.2, 1.6], jnp.float32)
    base = jnp.clip(jax.random.normal(key, (3, NATOM), jnp.float32), -5.0, 5.0)
    return scales[:, None] * ramp[None, :] * base + offset


def draw_mean_xyz(key, part):
    shape_mean = mean_shape(key)
    return shape_mean


def draw_frames_xyz(key, part):
    shape_mean = mean_shape(key)
    key = jax.random.fold_in(key, 2)
    keys = jax.random.split(key, 5)
    alpha = jax.random.uniform(keys[0], (FRAMES,), jnp.float32, -3.14159, 3.14159)
    beta = jax.random.uniform(keys[1], (FRAMES,), jnp.float32, -3.14159, 3.14159)
    gamma = jax.random.uniform(keys[2], (FRAMES,), jnp.float32, -3.14159, 3.14159)
    shift = 2.0 * jnp.clip(jax.random.normal(keys[3], (FRAMES, 3), jnp.float32), -5.0, 5.0)
    noise = 0.6 * jnp.clip(jax.random.normal(keys[4], (FRAMES, 3, NATOM), jnp.float32), -5.0, 5.0)
    ca, sa = (jnp.cos(alpha), jnp.sin(alpha))
    cb, sb = (jnp.cos(beta), jnp.sin(beta))
    cc, sc = (jnp.cos(gamma), jnp.sin(gamma))
    rows = [[ca * cb, ca * sb * sc - sa * cc, ca * sb * cc + sa * sc], [sa * cb, sa * sb * sc + ca * cc, sa * sb * cc - ca * sc], [-sb, cb * sc, cb * cc]]
    parts_list = []
    for irow in range(3):
        value = rows[irow][0][:, None] * shape_mean[0][None, :]
        value = value + rows[irow][1][:, None] * shape_mean[1][None, :]
        value = value + rows[irow][2][:, None] * shape_mean[2][None, :]
        parts_list.append(value + shift[:, irow][:, None])
    coords = jnp.stack(parts_list, axis=1) + noise
    return coords.astype(jnp.bfloat16)


def levels(rng, extent, cuts, low, top_value):
    gain = 1.0
    for axis_at, parts in cuts:
        heights = jax.random.uniform(jax.random.fold_in(jax.random.fold_in(rng, 6), axis_at), (parts,), jnp.float32, low / len(cuts), top_value / len(cuts))
        gain = gain * jnp.repeat(jnp.exp(heights), extent[axis_at] // parts).reshape((-1,) + (1,) * (len(extent) - 1 - axis_at))
    return gain


def normal_values(own_key, shape, scale, most, cuts=(), held_as=jnp.bfloat16):
    entries = jax.random.normal(own_key, shape, jnp.float32) * scale
    if len(cuts) > 0:
        entries = levels(own_key, shape, cuts, -0.22, 0.18) * entries
    return jnp.clip(entries, min=-most, max=most).astype(held_as)


def setup_inputs(seed: int = 0) -> dict:
    streams_of = jax.random.split(jax.random.key(seed), 4)
    frames_xyz = draw_frames_xyz(jax.random.fold_in(streams_of[3], 71), 0)
    mean_xyz = draw_mean_xyz(jax.random.fold_in(streams_of[3], 71), 0)
    vector_block = normal_values(streams_of[2], (K, 3, NATOM), 1.0, 6.0, ((2, 512),))
    return {"frames_xyz": frames_xyz, "mean_xyz": mean_xyz, "vector_block": vector_block}


def polar_factor(amat):
    for step in range(NS_STEPS):
        square = jnp.einsum('ijf,kjf->ikf', amat, amat, precision=lax.Precision.HIGHEST)
        amat = 1.5 * amat - 0.5 * jnp.einsum('ikf,kjf->ijf', square, amat, precision=lax.Precision.HIGHEST)
    return amat

def reference(frames_xyz, mean_xyz, vector_block):
    centre = lax.optimization_barrier(jnp.sum(mean_xyz, axis=1)) / NATOM
    centered_mean = mean_xyz - centre[:, None]
    block_size = math.gcd(FRAMES, 256)
    count = FRAMES // block_size
    vectors = vector_block.astype(jnp.float32)

    def one_block(total, index):
        start = (index * block_size).astype(jnp.int32)
        coords = lax.dynamic_slice_in_dim(frames_xyz, start, block_size, 0).astype(jnp.float32)
        sums = lax.optimization_barrier(jnp.sum(coords, axis=2))
        cross = jnp.einsum('fja,ia->ijf', coords, mean_xyz, precision=lax.Precision.HIGHEST)
        cross = cross - centre[:, None, None] * sums.T[None, :, :]
        scale_frob = jnp.sqrt(1.0 + lax.optimization_barrier(jnp.sum(cross * cross, axis=(0, 1))))
        rotation = polar_factor(cross / scale_frob[None, None, :])
        shifted = coords - (sums / NATOM)[:, :, None]
        deviation = jnp.einsum('ijf,fja->fia', rotation, shifted, precision=lax.Precision.HIGHEST)
        deviation = (deviation - centered_mean[None]).astype(jnp.bfloat16).astype(jnp.float32)
        projection = jnp.einsum('fia,kia->fk', deviation, vectors, precision=lax.Precision.HIGHEST)
        projection = projection.astype(jnp.bfloat16).astype(jnp.float32)
        total = total + jnp.einsum('fk,fia->kia', projection, deviation, precision=lax.Precision.HIGHEST)
        return (total, None)
    init = jnp.zeros((K, 3, NATOM), jnp.float32)
    total, unused = lax.scan(one_block, init, jnp.arange(count, dtype=jnp.int32))
    return total / FRAMES
```

```python
import functools

import jax
import jax.numpy as jnp
from jax import lax
from jax.experimental import pallas as pl
from jax.experimental.pallas import tpu as pltpu
from jax.sharding import Mesh
from jax.sharding import PartitionSpec as P

NS_STEPS = 8
LANES = 128
PAIR = 256
EXTRA = 16
F32 = jnp.float32
BF16 = jnp.bfloat16
HIGHEST = lax.Precision.HIGHEST
NT = (((1,), (1,)), ((), ()))
TN = (((0,), (0,)), ((), ()))


def iota(shape, dim):
    return lax.broadcasted_iota(jnp.int32, shape, dim)


def split3(value):
    high = value.astype(BF16)
    rest = value - high.astype(F32)
    middle = rest.astype(BF16)
    low = (rest - middle.astype(F32)).astype(BF16)
    return high, middle, low


def mean_rows(mean16):
    high, middle, low = split3(mean16)
    row = iota(mean16.shape, 0)
    take = jnp.where(row < 3, high.astype(F32), jnp.where(row < 6, middle.astype(F32), jnp.where(row < 9, low.astype(F32), mean16)))
    return take.astype(BF16)


def cross_kernel(core_ref, x_ref, mean_ref, keep_ref, send_ref, rows_ref, cross_ref, acc_ref):
    step = pl.program_id(0)
    core = core_ref[0]
    extra = mean_rows(mean_ref[...])
    width = x_ref.shape[1]

    @pl.when(step == 0)
    def _():
        acc_ref[...] = jnp.zeros_like(acc_ref)

    total = acc_ref[...]
    for pair in range(width // PAIR):
        columns = slice(pair * PAIR, (pair + 1) * PAIR)
        side = extra[:, columns]
        left = jnp.concatenate([x_ref[:, columns], side], axis=0)
        total += lax.dot_general(left, side, NT, preferred_element_type=F32)
        block = slice(pair * LANES, (pair + 1) * LANES)
        first, second = left[:-EXTRA, :LANES], left[:-EXTRA, LANES:]
        keep_ref[:, block] = jnp.where(core == 0, first, second)
        send_ref[:, block] = jnp.where(core == 0, second, first)
        rows_ref[:, block] = jnp.where(core == 0, side[:, :LANES], side[:, LANES:])
    acc_ref[...] = total

    @pl.when(step == pl.num_programs(0) - 1)
    def _():
        row, col = iota((8, EXTRA), 0), iota((8, EXTRA), 1)
        pick = ((row < 3) & (col < 9) & ((col == row) | (col == row + 3) | (col == row + 6))) | ((row == 3) & (col == 9))
        cross_ref[...] = lax.dot_general(pick.astype(F32), total, NT, precision=HIGHEST, preferred_element_type=F32)


def polar_factor(amat):
    for _ in range(NS_STEPS):
        square = [[sum(amat[i][j] * amat[k][j] for j in range(3)) for k in range(3)] for i in range(3)]
        amat = [[1.5 * amat[i][j] - 0.5 * sum(square[i][k] * amat[k][j] for k in range(3)) for j in range(3)] for i in range(3)]
    return amat


def rotation_kernel(natom, core_ref, parts_ref, out_ref):
    core = core_ref[0]
    half = parts_ref.shape[0] // 2
    frames = (parts_ref.shape[2] - EXTRA) // 3
    lanes = out_ref.shape[1]
    first, second = parts_ref[0], parts_ref[half]
    for index in range(1, half):
        first += parts_ref[index]
        second += parts_ref[half + index]
    own = jnp.where(core == 0, first, second)
    other = jnp.where(core == 0, second, first)
    row, lane = iota((EXTRA, lanes), 0), iota((EXTRA, lanes), 1)
    third = lanes // 3
    which = (lane >= third).astype(jnp.int32) + (lane >= 2 * third).astype(jnp.int32)
    ones_at = 3 * frames + 9
    centre = [own[i : i + 1, ones_at : ones_at + 1] / natom for i in range(3)]
    for side, total in enumerate((own, other)):
        sums = [total[3:4, j * frames : (j + 1) * frames] for j in range(3)]
        cross = [[total[i : i + 1, j * frames : (j + 1) * frames] - centre[i] * sums[j] for j in range(3)] for i in range(3)]
        scale = jnp.sqrt(1.0 + sum(cross[i][j] * cross[i][j] for i in range(3) for j in range(3)))
        rotation = polar_factor([[cross[i][j] / scale for j in range(3)] for i in range(3)])
        shift = [sum(rotation[i][j] * (sums[j] / natom) for j in range(3)) for i in range(3)]
        entries = [rotation[i][j] for i in range(3) for j in range(3)] + shift
        at = iota((EXTRA, frames), 0)
        packed = jnp.zeros((EXTRA, frames), F32)
        for index, entry in enumerate(entries):
            packed = jnp.where(at == index, entry, packed)
        for index in range(4):
            chosen = (row == 3 * which + index) if index < 3 else (row == 9 + which)
            spread = lax.dot_general(packed, chosen.astype(F32), TN, precision=HIGHEST, preferred_element_type=F32)
            begin = (2 * index + side) * frames
            out_ref[begin : begin + frames, :] = spread
    which8 = which[:8]
    out_ref[8 * frames : 8 * frames + 8, :] = jnp.where(which8 == 0, centre[0], jnp.where(which8 == 1, centre[1], centre[2]))


def lane_part(shape):
    lane = iota(shape, 1)
    third = shape[1] // 3
    return (lane >= third).astype(jnp.int32) + (lane >= 2 * third).astype(jnp.int32)


def projection_kernel(core_ref, keep_ref, recv_ref, rows_ref, vec_ref, rot_ref, out_ref, acc_ref):
    step = pl.program_id(0)
    core = core_ref[0]

    @pl.when(step == 0)
    def _():
        acc_ref[...] = jnp.zeros_like(acc_ref)

    total = acc_ref[...]
    for pair in range(keep_ref.shape[1] // PAIR):
        columns = slice(pair * PAIR, (pair + 1) * PAIR)
        left = jnp.concatenate([keep_ref[:, columns], recv_ref[:, columns], rows_ref[:, columns]], axis=0)
        right = jnp.concatenate([vec_ref[2 * pair], vec_ref[2 * pair + 1]], axis=1)
        total += lax.dot_general(left, right, NT, preferred_element_type=F32)
    acc_ref[...] = total

    @pl.when(step == pl.num_programs(0) - 1)
    def _():
        frames = keep_ref.shape[0] // 3
        lanes = vec_ref.shape[1]
        third = lanes // 3
        extra = total[6 * frames :, :]
        vec_sums = extra[9:10, :]
        centre = rot_ref[8 * frames : 8 * frames + 1, :]
        part = lane_part((1, lanes))
        along = [extra[i : i + 1] + extra[3 + i : 4 + i] + extra[6 + i : 7 + i] for i in range(3)]
        mean_term = jnp.where(part == 0, along[0], jnp.where(part == 1, along[1], along[2])) - centre * vec_sums
        halves = []
        for side in range(2):
            value = -rot_ref[(6 + side) * frames : (7 + side) * frames, :] * vec_sums - mean_term
            for j in range(3):
                spread = rot_ref[(2 * j + side) * frames : (2 * j + side + 1) * frames, :]
                begin = (3 * side + j) * frames
                value += spread * total[begin : begin + frames, :]
            halves.append(value)
        first = jnp.where(core == 0, halves[0], halves[1])
        second = jnp.where(core == 0, halves[1], halves[0])
        value = jnp.concatenate([first, second], axis=0)
        quarter = frames // 2
        row, col = iota((lanes, 4 * third), 0), iota((lanes, 4 * third), 1)
        packed = jnp.zeros((quarter, 4 * third), F32)
        for q in range(4):
            fold = (row % third == col % third) & (col // third == q)
            packed += lax.dot_general(
                value[q * quarter : (q + 1) * quarter, :], fold.astype(F32), (((1,), (0,)), ((), ())),
                precision=HIGHEST, preferred_element_type=F32,
            )
        out_ref[...] = packed


def product_kernel(core_ref, parts_ref, rot_ref, keep_ref, recv_ref, rows_ref, out_ref, weight_ref):
    step = pl.program_id(0)
    frames = keep_ref.shape[0] // 3
    lanes = rot_ref.shape[1]
    third = lanes // 3

    @pl.when(step == 0)
    def _():
        core = core_ref[0]
        packed = parts_ref[0]
        for index in range(1, parts_ref.shape[0]):
            packed += parts_ref[index]
        packed = packed.astype(BF16)
        row, col = iota((4 * third, lanes), 0), iota((4 * third, lanes), 1)
        quarters = []
        for q in range(4):
            unfold = (row % third == col % third) & (row // third == q)
            quarters.append(jnp.dot(packed, unfold.astype(F32).astype(BF16), preferred_element_type=F32))
        first = jnp.concatenate(quarters[:2], axis=0)
        second = jnp.concatenate(quarters[2:], axis=0)
        sides = (jnp.where(core == 0, first, second), jnp.where(core == 0, second, first))
        centre = rot_ref[8 * frames : 8 * frames + 1, :]
        pieces = []
        proj_sum = jnp.zeros((1, lanes), F32)
        shift_sum = jnp.zeros((1, lanes), F32)
        for side in range(2):
            for j in range(3):
                begin = (2 * j + side) * frames
                pieces.append(rot_ref[begin : begin + frames, :] * sides[side])
            proj_sum += jnp.sum(sides[side], axis=0, keepdims=True)
            shift = rot_ref[(6 + side) * frames : (7 + side) * frames, :]
            shift_sum += jnp.sum(sides[side] * shift, axis=0, keepdims=True)
        at, part = iota((EXTRA, lanes), 0), lane_part((EXTRA, lanes))
        is_mean = (at < 9) & ((at == part) | (at == part + 3) | (at == part + 6))
        tail = jnp.where(is_mean, -proj_sum, jnp.where(at == 9, centre * proj_sum - shift_sum, 0.0))
        weight = jnp.concatenate(pieces + [tail], axis=0)
        same = (iota((lanes, lanes), 0) == iota((lanes, lanes), 1)).astype(F32).astype(BF16)
        for index, piece in enumerate(split3(weight)):
            turned = lax.dot_general(same, piece, NT, preferred_element_type=F32)
            weight_ref[index * lanes : (index + 1) * lanes, :] = turned.astype(BF16)

    weight = weight_ref[...]
    for pair in range(keep_ref.shape[1] // PAIR):
        columns = slice(pair * PAIR, (pair + 1) * PAIR)
        right = jnp.concatenate([keep_ref[:, columns], recv_ref[:, columns], rows_ref[:, columns]], axis=0)
        term = jnp.dot(weight, right, preferred_element_type=F32)
        term = (term[2 * lanes :] + term[lanes : 2 * lanes] + term[:lanes]).astype(BF16)
        out_ref[2 * pair] = term[:, :LANES]
        out_ref[2 * pair + 1] = term[:, LANES:]


VMEM_LIMIT = 40 * 1024 * 1024
SMEM_SPEC = pl.BlockSpec(memory_space=pltpu.SMEM)


def params():
    return pltpu.CompilerParams(vmem_limit_bytes=VMEM_LIMIT, dimension_semantics=("arbitrary",))


def cost(flops, moved):
    return pl.CostEstimate(flops=flops, bytes_accessed=moved, transcendentals=0)


def whole(*shape):
    return pl.BlockSpec(shape, lambda step: (0,) * len(shape))


def body(frames_xyz, mean_xyz, vector_block):
    frames, _, atoms = frames_xyz.shape
    kcount, _, own_atoms = vector_block.shape
    lanes = 3 * kcount
    rows = 3 * frames
    half = atoms // 2
    chips = half // own_atoms
    coords_size = lax.axis_size("yl") * lax.axis_size("x")
    peers = 2 * coords_size
    natom = atoms * coords_size
    frame_count = frames * 2 * chips
    core = lax.axis_index("core").astype(jnp.int32).reshape(1)
    x_rows = frames_xyz.transpose(1, 0, 2).reshape(rows, atoms)
    vec_rows = vector_block.transpose(1, 0, 2).reshape(lanes, own_atoms)
    vecs = lax.all_to_all(
        jnp.broadcast_to(vec_rows[None], (chips, lanes, own_atoms)), ("z", "yh"), 0, 0, tiled=True
    )
    mean16 = jnp.concatenate([mean_xyz] * 3 + [jnp.ones((1, atoms), F32), jnp.zeros((EXTRA - 10, atoms), F32)], axis=0)

    steps = max(1, atoms // 2048)
    wide, narrow = atoms // steps, half // steps
    columns = lambda height, width: pl.BlockSpec((height, width), lambda step: (0, step))
    keep, send, side, cross = pl.pallas_call(
        cross_kernel,
        grid=(steps,),
        in_specs=[SMEM_SPEC, columns(rows, wide), columns(EXTRA, wide)],
        out_specs=[columns(rows, narrow), columns(rows, narrow), columns(EXTRA, narrow), whole(8, rows + EXTRA)],
        out_shape=[
            jax.ShapeDtypeStruct((rows, half), BF16),
            jax.ShapeDtypeStruct((rows, half), BF16),
            jax.ShapeDtypeStruct((EXTRA, half), BF16),
            jax.ShapeDtypeStruct((8, rows + EXTRA), F32),
        ],
        scratch_shapes=[pltpu.VMEM((rows + EXTRA, EXTRA), F32)],
        compiler_params=params(),
        cost_estimate=cost(2 * rows * atoms * 256, 4 * rows * atoms),
        name="cross_terms",
    )(core, x_rows, mean16)
    recv = lax.ppermute(send, "core", [(0, 1), (1, 0)])
    parts = lax.all_to_all(
        jnp.broadcast_to(cross[None], (peers,) + cross.shape), ("core", "yl", "x"), 0, 0, tiled=True
    )
    rot = pl.pallas_call(
        functools.partial(rotation_kernel, natom),
        grid=(1,),
        in_specs=[SMEM_SPEC, whole(*parts.shape)],
        out_specs=whole(8 * frames + 8, lanes),
        out_shape=jax.ShapeDtypeStruct((8 * frames + 8, lanes), F32),
        compiler_params=params(),
        cost_estimate=cost(10**9, 10**6),
        name="rotation",
    )(core, parts)

    blocks = chips // steps
    vec_spec = pl.BlockSpec((blocks, lanes, LANES), lambda step: (step, 0, 0))
    proj = pl.pallas_call(
        projection_kernel,
        grid=(steps,),
        in_specs=[SMEM_SPEC, columns(rows, narrow), columns(rows, narrow), columns(EXTRA, narrow), vec_spec, whole(*rot.shape)],
        out_specs=whole(frames // 2, 4 * kcount),
        out_shape=jax.ShapeDtypeStruct((frames // 2, 4 * kcount), F32),
        scratch_shapes=[pltpu.VMEM((2 * rows + EXTRA, lanes), F32)],
        compiler_params=params(),
        cost_estimate=cost(4 * rows * half * 256, 4 * rows * half),
        name="projection",
    )(core, keep, recv, side, vecs, rot)
    proj_parts = lax.all_to_all(
        jnp.broadcast_to(proj[None], (peers,) + proj.shape), ("core", "yl", "x"), 0, 0, tiled=True
    )
    term = pl.pallas_call(
        product_kernel,
        grid=(steps,),
        in_specs=[
            SMEM_SPEC, whole(*proj_parts.shape), whole(*rot.shape),
            columns(rows, narrow), columns(rows, narrow), columns(EXTRA, narrow),
        ],
        out_specs=vec_spec,
        out_shape=jax.ShapeDtypeStruct((chips, lanes, LANES), BF16),
        scratch_shapes=[pltpu.VMEM((3 * lanes, 2 * rows + EXTRA), BF16)],
        compiler_params=params(),
        cost_estimate=cost(4 * rows * half * 288, 4 * rows * half),
        name="product_terms",
    )(core, proj_parts, rot, keep, recv, side)
    terms = lax.all_to_all(term, ("z", "yh"), 0, 0, tiled=True)
    total = jnp.sum(terms.astype(F32), axis=0) / frame_count
    return total.reshape(3, kcount, own_atoms).transpose(1, 0, 2)


def solution(mesh):
    sizes = mesh_sizes(mesh)
    inner = Mesh(mesh.devices.reshape(sizes), ("z", "yh", "core", "yl", "x"))
    frames, coords = ("z", "yh", "core"), ("yl", "x")
    in_specs = (P(frames, None, coords), P(None, coords), P(None, None, coords + frames))
    out_specs = P(None, None, coords + frames)
    return jax.shard_map(body, mesh=inner, in_specs=in_specs, out_specs=out_specs, check_vma=False)


def mesh_sizes(mesh):
    frames, coords = mesh.shape["frames"], mesh.shape["coords"]
    return (frames // 8, 4, 2, 2, coords // 2)
```

```python
import functools

import jax
import jax.numpy as jnp
from jax import lax
from jax.experimental import pallas as pl
from jax.experimental.pallas import tpu as pltpu
from jax.sharding import Mesh
from jax.sharding import PartitionSpec as P

NS_STEPS = 8
LANES = 128
PAIR = 256
EXTRA = 16
F32 = jnp.float32
BF16 = jnp.bfloat16
HIGHEST = lax.Precision.HIGHEST
NT = (((1,), (1,)), ((), ()))
TN = (((0,), (0,)), ((), ()))


def iota(shape, dim):
    return lax.broadcasted_iota(jnp.int32, shape, dim)


def split3(value):
    high = value.astype(BF16)
    rest = value - high.astype(F32)
    middle = rest.astype(BF16)
    low = (rest - middle.astype(F32)).astype(BF16)
    return high, middle, low


def mean_rows(mean):
    shape = (EXTRA, mean.shape[1])
    row = iota(shape, 0)
    spread = jnp.where(row == 9, 1.0, 0.0)
    for i in range(3):
        spread = jnp.where((row < 9) & (row % 3 == i), mean[i : i + 1, :], spread)
    high, middle, low = split3(spread)
    take = jnp.where((row >= 3) & (row < 6), middle.astype(F32), jnp.where((row >= 6) & (row < 9), low.astype(F32), high.astype(F32)))
    return take.astype(BF16)


def cross_kernel(place_ref, x_ref, mean_ref, keep_ref, send_ref, rows_ref, cross_ref, acc_ref):
    step = pl.program_id(0)
    parity, core = place_ref[0], place_ref[1]
    extra = mean_rows(mean_ref[...])
    width = x_ref.shape[1]

    @pl.when(step == 0)
    def _():
        acc_ref[...] = jnp.zeros_like(acc_ref)

    total = acc_ref[...]
    pairs = width // PAIR
    for pair in range(pairs):
        columns = slice(pair * PAIR, (pair + 1) * PAIR)
        side = extra[:, columns]
        left = jnp.concatenate([x_ref[:, columns], side], axis=0)
        total += lax.dot_general(left, side, NT, preferred_element_type=F32)
        block = slice(pair % (pairs // 2) * LANES, (pair % (pairs // 2) + 1) * LANES)
        first, second = left[:, :LANES], left[:, LANES:]
        mine = jnp.where(core == 0, first, second)
        theirs = jnp.where(core == 0, second, first)
        other = (parity + pair // (pairs // 2)) % 2
        keep_ref[other, :, block] = mine[:-EXTRA]
        send_ref[other, :, block] = theirs[:-EXTRA]
        rows_ref[other, :, block] = mine[-EXTRA:]
    acc_ref[...] = total

    @pl.when(step == pl.num_programs(0) - 1)
    def _():
        row, col = iota((8, EXTRA), 0), iota((8, EXTRA), 1)
        pick = ((row < 3) & (col < 9) & ((col == row) | (col == row + 3) | (col == row + 6))) | ((row == 3) & (col == 9))
        cross = lax.dot_general(pick.astype(F32), total, NT, precision=HIGHEST, preferred_element_type=F32)
        cross_ref[...] = jnp.broadcast_to(cross[None], cross_ref.shape)


def polar_factor(amat):
    for _ in range(NS_STEPS):
        square = [[sum(amat[i][j] * amat[k][j] for j in range(3)) for k in range(3)] for i in range(3)]
        amat = [[1.5 * amat[i][j] - 0.5 * sum(square[i][k] * amat[k][j] for k in range(3)) for j in range(3)] for i in range(3)]
    return amat


def rotation_kernel(natom, core_ref, parts_ref, gram_ref, out_ref, proj_ref):
    half = parts_ref.shape[0] // 2
    frames = (parts_ref.shape[2] - EXTRA) // 3
    lanes = out_ref.shape[1]
    first, second = parts_ref[0], parts_ref[half]
    for index in range(1, half):
        first += parts_ref[index]
        second += parts_ref[half + index]
    is_first = core_ref[0] == 0
    own = jnp.where(is_first, first, second)
    other = jnp.where(is_first, second, first)
    ones_at = 3 * frames + 9
    centre = [own[i : i + 1, ones_at : ones_at + 1] / natom for i in range(3)]
    columns = [[total[:, j * frames : (j + 1) * frames] for total in (own, other)] for j in range(3)]
    row = lambda index, j: jnp.concatenate([part[index : index + 1] for part in columns[j]], axis=0)
    sums = [row(3, j) for j in range(3)]
    cross = [[row(i, j) - centre[i] * sums[j] for j in range(3)] for i in range(3)]
    scale = jnp.sqrt(1.0 + sum(cross[i][j] * cross[i][j] for i in range(3) for j in range(3)))
    rotation = polar_factor([[cross[i][j] / scale for j in range(3)] for i in range(3)])
    shift = [sum(rotation[i][j] * (sums[j] / natom) for j in range(3)) for i in range(3)]
    entries = [rotation[i][j] for i in range(3) for j in range(3)] + shift
    at = iota((EXTRA, frames), 0)
    index3, lane = iota((3 * EXTRA, 4 * LANES), 0) % EXTRA, iota((3 * EXTRA, 4 * LANES), 1)
    third = lanes // 3
    place, within = lane // LANES, lane % LANES
    which = within // third
    chosen = ((place < 3) & (index3 == 3 * which + place)) | ((place == 3) & (index3 == 9 + which))
    chosen = jnp.where(chosen & (which < 3), 1.0, 0.0).astype(BF16)
    for side in range(2):
        packed = jnp.zeros((EXTRA, frames), F32)
        for index, entry in enumerate(entries):
            packed = jnp.where(at == index, entry[side : side + 1], packed)
        pieces = jnp.concatenate([piece.astype(F32) for piece in split3(packed)], axis=0).astype(BF16)
        spread = lax.dot_general(pieces, chosen, TN, preferred_element_type=F32)
        for index in range(4):
            begin = (2 * index + side) * frames
            out_ref[begin : begin + frames, :] = spread[:, index * LANES : index * LANES + lanes]
    which8 = lane_part((8, lanes))
    out_ref[8 * frames : 8 * frames + 8, :] = jnp.where(which8 == 0, centre[0], jnp.where(which8 == 1, centre[1], centre[2]))
    proj = packed_projection(is_first, gram_ref, out_ref, frames)
    proj_ref[...] = jnp.broadcast_to(proj[None], proj_ref.shape)


def lane_part(shape):
    lane = iota(shape, 1)
    third = shape[1] // 3
    return (lane >= third).astype(jnp.int32) + (lane >= 2 * third).astype(jnp.int32)


def fetch(refs, buffers, sems, others, chunks):
    width = refs[0].shape[2] // chunks
    copies = []
    for index, other in enumerate(others):
        for chunk in range(chunks):
            columns = pl.ds(chunk * width, width)
            group = []
            for which, (ref, buffer) in enumerate(zip(refs, buffers)):
                copy = pltpu.make_async_copy(
                    ref.at[other, :, columns], buffer.at[index, :, columns], sems.at[which, index * chunks + chunk]
                )
                copy.start()
                group.append(copy)
            copies.append(group)
    return copies


def halves_kernel(same_ref, up_ref, down_ref):
    half = up_ref.shape[1]
    up_ref[...] = same_ref[:, :half]
    down_ref[...] = same_ref[:, half:]


def gram_kernel(keep_hbm, recv_hbm, rows_ref, same_ref, below_ref, above_ref, out_ref, keep_ref, recv_ref, sems):
    chunks = sems.shape[1] // 2
    copies = fetch((keep_hbm, recv_hbm), (keep_ref, recv_ref), sems, (0, 1), chunks)
    total = jnp.zeros(out_ref.shape, F32)
    pairs = same_ref.shape[0] // 2
    for other in range(2):
        for pair in range(pairs):
            if pair % (pairs // chunks) == 0:
                for copy in copies[other * chunks + pair // (pairs // chunks)]:
                    copy.wait()
            columns = slice(pair * PAIR, (pair + 1) * PAIR)
            left = jnp.concatenate([ref[other, :, columns] for ref in (keep_ref, recv_ref, rows_ref)], axis=0)
            ref, at = (same_ref, 2 * pair) if other == 0 else ((below_ref, above_ref)[pair % 2], pair // 2 * 2)
            right = jnp.concatenate([ref[at], ref[at + 1]], axis=1)
            total += lax.dot_general(left, right, NT, preferred_element_type=F32)
    out_ref[...] = total


def packed_projection(is_first, gram_ref, rot_ref, frames):
    lanes = gram_ref.shape[1]
    third = lanes // 3
    extra = gram_ref[6 * frames :, :]
    vec_sums = extra[9:10, :]
    centre = rot_ref[8 * frames : 8 * frames + 1, :]
    part = lane_part((1, lanes))
    along = [extra[i : i + 1] + extra[3 + i : 4 + i] + extra[6 + i : 7 + i] for i in range(3)]
    mean_term = jnp.where(part == 0, along[0], jnp.where(part == 1, along[1], along[2])) - centre * vec_sums
    halves = []
    for side in range(2):
        value = -rot_ref[(6 + side) * frames : (7 + side) * frames, :] * vec_sums - mean_term
        for j in range(3):
            spread = rot_ref[(2 * j + side) * frames : (2 * j + side + 1) * frames, :]
            begin = (3 * side + j) * frames
            value += spread * gram_ref[begin : begin + frames, :]
        halves.append(value)
    first = jnp.where(is_first, halves[0], halves[1])
    second = jnp.where(is_first, halves[1], halves[0])
    value = jnp.concatenate([first, second], axis=0)
    quarter = frames // 2
    row, col = iota((lanes, 4 * third), 0), iota((lanes, 4 * third), 1)
    packed = jnp.zeros((quarter, 4 * third), F32)
    pieces = split3(value)
    for q in range(4):
        fold = jnp.where((row % third == col % third) & (col // third == q), 1.0, 0.0).astype(BF16)
        for piece in pieces:
            packed += jnp.dot(piece[q * quarter : (q + 1) * quarter, :], fold, preferred_element_type=F32)
    return packed


def product_weights(is_first, parts_ref, rot_ref, weight_ref, frames, scale):
    lanes = rot_ref.shape[1]
    third = lanes // 3

    packed = parts_ref[0]
    for index in range(1, parts_ref.shape[0]):
        packed += parts_ref[index]
    packed = packed.astype(BF16)
    row, col = iota((4 * third, lanes), 0), iota((4 * third, lanes), 1)
    quarters = []
    for q in range(4):
        unfold = (row % third == col % third) & (row // third == q)
        quarters.append(jnp.dot(packed, unfold.astype(F32).astype(BF16), preferred_element_type=F32))
    first = jnp.concatenate(quarters[:2], axis=0)
    second = jnp.concatenate(quarters[2:], axis=0)
    sides = (jnp.where(is_first, first, second), jnp.where(is_first, second, first))
    centre = rot_ref[8 * frames : 8 * frames + 1, :]
    pieces = []
    proj_sum = jnp.zeros((1, lanes), F32)
    shift_sum = jnp.zeros((1, lanes), F32)
    for side in range(2):
        for j in range(3):
            begin = (2 * j + side) * frames
            pieces.append(rot_ref[begin : begin + frames, :] * sides[side])
        proj_sum += jnp.sum(sides[side], axis=0, keepdims=True)
        shift = rot_ref[(6 + side) * frames : (7 + side) * frames, :]
        shift_sum += jnp.sum(sides[side] * shift, axis=0, keepdims=True)
    at, part = iota((EXTRA, lanes), 0), lane_part((EXTRA, lanes))
    is_mean = (at < 9) & ((at == part) | (at == part + 3) | (at == part + 6))
    tail = jnp.where(is_mean, -proj_sum, jnp.where(at == 9, centre * proj_sum - shift_sum, 0.0))
    weight = jnp.concatenate(pieces + [tail], axis=0) * scale
    same = (iota((lanes, lanes), 0) == iota((lanes, lanes), 1)).astype(F32).astype(BF16)
    for index, piece in enumerate(split3(weight)):
        turned = lax.dot_general(same, piece, NT, preferred_element_type=F32)
        weight_ref[index * lanes : (index + 1) * lanes, :] = turned.astype(BF16)


def weighted(weight, refs, columns):
    term = jnp.dot(weight, jnp.concatenate([ref[0, :, columns] for ref in refs], axis=0), preferred_element_type=F32)
    lanes = term.shape[0] // 3
    return term[2 * lanes :] + term[lanes : 2 * lanes] + term[:lanes]


def product_kernel(
    scale, core_ref, parts_ref, rot_ref, keep_hbm, recv_hbm, rows_ref, up_ref, down_ref, weight_ref, keep_ref, recv_ref, sems
):
    chunks = sems.shape[1]
    copies = fetch((keep_hbm, recv_hbm), (keep_ref, recv_ref), sems, (1,), chunks)
    product_weights(core_ref[0] == 0, parts_ref, rot_ref, weight_ref, keep_ref.shape[1] // 3, scale)
    weight = weight_ref[...]
    pairs = up_ref.shape[0]
    for pair in range(pairs):
        if pair % (pairs // chunks) == 0:
            for copy in copies[pair // (pairs // chunks)]:
                copy.wait()
        columns = slice(pair * PAIR, (pair + 1) * PAIR)
        term = weighted(weight, (keep_ref, recv_ref, rows_ref.at[pl.ds(1, 1)]), columns).astype(BF16)
        out_ref = (up_ref, down_ref)[pair % 2]
        out_ref[pair // 2 * 2] = term[:, :LANES]
        out_ref[pair // 2 * 2 + 1] = term[:, LANES:]


def product_same_kernel(weight_ref, keep_ref, recv_ref, rows_ref, out_ref):
    weight = weight_ref[...]
    for pair in range(out_ref.shape[0] // 2):
        term = weighted(weight, (keep_ref, recv_ref, rows_ref), slice(pair * PAIR, (pair + 1) * PAIR))
        out_ref[2 * pair] = term[:, :LANES]
        out_ref[2 * pair + 1] = term[:, LANES:]


MIB = 1024 * 1024
GRAM_FLOPS = 10000000000
ROTATION_FLOPS = 10**9
HALVES_FLOPS = 20000000000
SMEM_SPEC = pl.BlockSpec(memory_space=pltpu.SMEM)


def params(limit=16):
    return pltpu.CompilerParams(vmem_limit_bytes=limit * MIB, dimension_semantics=("arbitrary",))


def cost(flops, moved):
    return pl.CostEstimate(flops=flops, bytes_accessed=moved, transcendentals=0)


def whole(*shape):
    return pl.BlockSpec(shape, lambda step: (0,) * len(shape))


def body(frames_xyz, mean_xyz, vector_block):
    frames, _, atoms = frames_xyz.shape
    kcount, _, own_atoms = vector_block.shape
    lanes = 3 * kcount
    rows = 3 * frames
    steps, quads = lax.axis_size("zh"), lax.axis_size("yh")
    chips = steps * quads
    peers = 2 * lax.axis_size("yl") * lax.axis_size("x")
    natom = atoms * lax.axis_size("yl") * lax.axis_size("x")
    frame_count = frames * 4 * chips
    ring = 2 * steps
    upward = [(i, (i + 1) % ring) for i in range(ring)]
    downward = [(i, (i - 1) % ring) for i in range(ring)]
    core = lax.axis_index("core").astype(jnp.int32).reshape(1)
    place = jnp.concatenate([lax.axis_index("zp").astype(jnp.int32).reshape(1), core])
    x_rows = frames_xyz.transpose(1, 0, 2).reshape(rows, atoms)
    vec_rows = vector_block.transpose(1, 0, 2).reshape(lanes, own_atoms)
    same = lax.all_to_all(
        jnp.broadcast_to(vec_rows[None], (chips, lanes, own_atoms)), ("zh", "yh"), 0, 0, tiled=True
    )

    wide, narrow = atoms // steps, atoms // steps // 4
    both = lambda height: pl.BlockSpec((2, height, narrow), lambda step: (0, 0, step))
    part = lambda height, which: pl.BlockSpec((1, height, narrow), lambda step: (which, 0, step))
    sorted_shape = lambda height: jax.ShapeDtypeStruct((2, height, steps * narrow), BF16)
    keep, send, side, cross = pl.pallas_call(
        cross_kernel,
        grid=(steps,),
        in_specs=[
            SMEM_SPEC,
            pl.BlockSpec((rows, wide), lambda step: (0, step)),
            pl.BlockSpec((3, wide), lambda step: (0, step)),
        ],
        out_specs=[both(rows), both(rows), both(EXTRA), whole(peers, 8, rows + EXTRA)],
        out_shape=[
            sorted_shape(rows), sorted_shape(rows), sorted_shape(EXTRA), jax.ShapeDtypeStruct((peers, 8, rows + EXTRA), F32),
        ],
        scratch_shapes=[pltpu.VMEM((rows + EXTRA, EXTRA), F32)],
        compiler_params=params(),
        cost_estimate=cost(2 * rows * atoms * 256, 4 * rows * atoms),
        name="cross_terms",
    )(place, x_rows, mean_xyz)
    recv = lax.ppermute(send, "core", [(0, 1), (1, 0)])
    cross, same = lax.optimization_barrier((cross, same))
    parts = lax.all_to_all(cross, ("core", "yl", "x"), 0, 0, tiled=True)
    shape = (chips // 2, lanes, own_atoms)
    vmem, hbm = pl.BlockSpec(memory_space=pltpu.VMEM), pl.BlockSpec(memory_space=pl.ANY)
    to_above, to_below = pl.pallas_call(
        halves_kernel,
        in_specs=[vmem],
        out_specs=[vmem, vmem],
        out_shape=[jax.ShapeDtypeStruct((steps, quads // 2, lanes, own_atoms), BF16)] * 2,
        compiler_params=pltpu.CompilerParams(vmem_limit_bytes=16 * MIB),
        cost_estimate=cost(HALVES_FLOPS, 10**6),
        name="vector_halves",
    )(same.reshape(steps, quads, lanes, own_atoms))
    below = lax.ppermute(to_above.reshape(shape), ("zh", "zp"), upward)
    above = lax.ppermute(to_below.reshape(shape), ("zh", "zp"), downward)
    blocks = lambda count: pl.BlockSpec((count, lanes, LANES), lambda step: (step, 0, 0))
    gram_rows = 2 * rows + EXTRA
    chunks = 2 if steps > 1 else 1
    gram = pl.pallas_call(
        gram_kernel,
        in_specs=[hbm, hbm, vmem, vmem, vmem, vmem],
        out_specs=vmem,
        out_shape=jax.ShapeDtypeStruct((gram_rows, lanes), F32),
        scratch_shapes=[pltpu.VMEM(keep.shape, BF16)] * 2 + [pltpu.SemaphoreType.DMA((2, 2 * chunks))],
        compiler_params=pltpu.CompilerParams(vmem_limit_bytes=16 * MIB),
        cost_estimate=cost(GRAM_FLOPS, 10**6),
        name="vector_products",
    )(keep, recv, side, same, below, above)
    rot_shape = (8 * frames + 8, lanes)
    rot, proj = pl.pallas_call(
        functools.partial(rotation_kernel, natom),
        in_specs=[SMEM_SPEC, vmem, vmem],
        out_specs=[vmem, vmem],
        out_shape=[
            jax.ShapeDtypeStruct(rot_shape, F32),
            jax.ShapeDtypeStruct((peers, frames // 2, 4 * kcount), F32),
        ],
        compiler_params=pltpu.CompilerParams(vmem_limit_bytes=16 * MIB),
        cost_estimate=cost(ROTATION_FLOPS, 10**6),
        name="rotation_projection",
    )(core, parts, gram)
    proj_parts = lax.all_to_all(proj, ("core", "yl", "x"), 0, 0, tiled=True)
    up, down, weight = pl.pallas_call(
        functools.partial(product_kernel, 1.0 / frame_count),
        in_specs=[SMEM_SPEC, vmem, vmem, hbm, hbm, vmem],
        out_specs=[vmem, vmem, vmem],
        out_shape=[
            jax.ShapeDtypeStruct(shape, BF16), jax.ShapeDtypeStruct(shape, BF16),
            jax.ShapeDtypeStruct((3 * lanes, gram_rows), BF16),
        ],
        scratch_shapes=[pltpu.VMEM((1, rows, steps * narrow), BF16)] * 2 + [pltpu.SemaphoreType.DMA((2, 2 * chunks))],
        compiler_params=pltpu.CompilerParams(vmem_limit_bytes=16 * MIB),
        cost_estimate=cost(1, 1),
        name="product_terms",
    )(core, proj_parts, rot, keep, recv, side)
    from_below = lax.ppermute(up, ("zh", "zp"), upward)
    from_above = lax.ppermute(down, ("zh", "zp"), downward)
    own = pl.pallas_call(
        product_same_kernel,
        grid=(steps,),
        in_specs=[whole(3 * lanes, gram_rows), part(rows, 0), part(rows, 0), part(EXTRA, 0)],
        out_specs=blocks(quads),
        out_shape=jax.ShapeDtypeStruct((chips, lanes, LANES), F32),
        compiler_params=params(),
        cost_estimate=cost(2 * rows * atoms * 256, 4 * rows * atoms),
        name="product_terms_same",
    )(weight, keep, recv, side)
    halves = (steps, quads // 2, lanes, own_atoms)
    neighbours = jnp.concatenate([from_below.reshape(halves), from_above.reshape(halves)], axis=1)
    term = (own + neighbours.reshape(own.shape).astype(F32)).astype(BF16)
    terms = lax.all_to_all(term, ("zh", "yh"), 0, 0, tiled=True)
    total = jnp.sum(terms.astype(F32), axis=0)
    return total.reshape(3, kcount, own_atoms).transpose(1, 0, 2)


def solution(mesh):
    inner = Mesh(mesh.devices.reshape(mesh_sizes(mesh)), ("zh", "zp", "yh", "core", "yl", "x"))
    frames, coords = ("zh", "zp", "yh", "core"), ("yl", "x")
    in_specs = (P(frames, None, coords), P(None, coords), P(None, None, coords + frames))
    out_specs = P(None, None, coords + frames)
    return jax.shard_map(body, mesh=inner, in_specs=in_specs, out_specs=out_specs, check_vma=False)


def mesh_sizes(mesh):
    frames, coords = mesh.shape["frames"], mesh.shape["coords"]
    return (frames // 16, 2, 4, 2, 2, coords // 2)
```

```python
import functools

import jax
import jax.numpy as jnp
from jax import lax
from jax.experimental import pallas as pl
from jax.experimental.pallas import tpu as pltpu
from jax.sharding import Mesh
from jax.sharding import PartitionSpec as P

NS_STEPS = 8
LANES = 128
PAIR = 256
EXTRA = 16
F32 = jnp.float32
BF16 = jnp.bfloat16
HIGHEST = lax.Precision.HIGHEST
NT = (((1,), (1,)), ((), ()))
TN = (((0,), (0,)), ((), ()))


def iota(shape, dim):
    return lax.broadcasted_iota(jnp.int32, shape, dim)


def split3(value):
    high = value.astype(BF16)
    rest = value - high.astype(F32)
    middle = rest.astype(BF16)
    low = (rest - middle.astype(F32)).astype(BF16)
    return high, middle, low


def mean_rows(mean):
    shape = (EXTRA, mean.shape[1])
    row = iota(shape, 0)
    spread = jnp.where(row == 9, 1.0, 0.0)
    for i in range(3):
        spread = jnp.where((row < 9) & (row % 3 == i), mean[i : i + 1, :], spread)
    high, middle, low = split3(spread)
    take = jnp.where((row >= 3) & (row < 6), middle.astype(F32), jnp.where((row >= 6) & (row < 9), low.astype(F32), high.astype(F32)))
    return take.astype(BF16)


def cross_kernel(place_ref, x_ref, mean_ref, keep_ref, send_ref, rows_ref, cross_ref, acc_ref):
    step = pl.program_id(0)
    parity, core = place_ref[0], place_ref[1]
    extra = mean_rows(mean_ref[...])
    width = x_ref.shape[1]

    @pl.when(step == 0)
    def _():
        acc_ref[...] = jnp.zeros_like(acc_ref)

    total = acc_ref[...]
    pairs = width // PAIR
    for pair in range(pairs):
        columns = slice(pair * PAIR, (pair + 1) * PAIR)
        side = extra[:, columns]
        left = jnp.concatenate([x_ref[:, columns], side], axis=0)
        total += lax.dot_general(left, side, NT, preferred_element_type=F32)
        block = slice(pair % (pairs // 2) * LANES, (pair % (pairs // 2) + 1) * LANES)
        first, second = left[:, :LANES], left[:, LANES:]
        mine = jnp.where(core == 0, first, second)
        theirs = jnp.where(core == 0, second, first)
        other = (parity + pair // (pairs // 2)) % 2
        keep_ref[other, :, block] = mine[:-EXTRA]
        send_ref[other, :, block] = theirs[:-EXTRA]
        rows_ref[other, :, block] = mine[-EXTRA:]
    acc_ref[...] = total

    @pl.when(step == pl.num_programs(0) - 1)
    def _():
        row, col = iota((8, EXTRA), 0), iota((8, EXTRA), 1)
        pick = ((row < 3) & (col < 9) & ((col == row) | (col == row + 3) | (col == row + 6))) | ((row == 3) & (col == 9))
        cross = lax.dot_general(pick.astype(F32), total, NT, precision=HIGHEST, preferred_element_type=F32)
        cross_ref[...] = jnp.broadcast_to(cross[None], cross_ref.shape)


def polar_factor(amat):
    for _ in range(NS_STEPS):
        square = [[sum(amat[i][j] * amat[k][j] for j in range(3)) for k in range(3)] for i in range(3)]
        amat = [[1.5 * amat[i][j] - 0.5 * sum(square[i][k] * amat[k][j] for k in range(3)) for j in range(3)] for i in range(3)]
    return amat


def rotation_kernel(natom, core_ref, parts_ref, gram_ref, out_ref, proj_ref):
    half = parts_ref.shape[0] // 2
    frames = (parts_ref.shape[2] - EXTRA) // 3
    lanes = out_ref.shape[1]
    first, second = parts_ref[0], parts_ref[half]
    for index in range(1, half):
        first += parts_ref[index]
        second += parts_ref[half + index]
    is_first = core_ref[0] == 0
    own = jnp.where(is_first, first, second)
    other = jnp.where(is_first, second, first)
    ones_at = 3 * frames + 9
    centre = [own[i : i + 1, ones_at : ones_at + 1] / natom for i in range(3)]
    columns = [[total[:, j * frames : (j + 1) * frames] for total in (own, other)] for j in range(3)]
    row = lambda index, j: jnp.concatenate([part[index : index + 1] for part in columns[j]], axis=0)
    sums = [row(3, j) for j in range(3)]
    cross = [[row(i, j) - centre[i] * sums[j] for j in range(3)] for i in range(3)]
    scale = jnp.sqrt(1.0 + sum(cross[i][j] * cross[i][j] for i in range(3) for j in range(3)))
    rotation = polar_factor([[cross[i][j] / scale for j in range(3)] for i in range(3)])
    shift = [sum(rotation[i][j] * (sums[j] / natom) for j in range(3)) for i in range(3)]
    entries = [rotation[i][j] for i in range(3) for j in range(3)] + shift
    at = iota((EXTRA, frames), 0)
    index3, lane = iota((3 * EXTRA, 4 * LANES), 0) % EXTRA, iota((3 * EXTRA, 4 * LANES), 1)
    third = lanes // 3
    place, within = lane // LANES, lane % LANES
    which = within // third
    chosen = ((place < 3) & (index3 == 3 * which + place)) | ((place == 3) & (index3 == 9 + which))
    chosen = jnp.where(chosen & (which < 3), 1.0, 0.0).astype(BF16)
    for side in range(2):
        packed = jnp.zeros((EXTRA, frames), F32)
        for index, entry in enumerate(entries):
            packed = jnp.where(at == index, entry[side : side + 1], packed)
        pieces = jnp.concatenate([piece.astype(F32) for piece in split3(packed)], axis=0).astype(BF16)
        spread = lax.dot_general(pieces, chosen, TN, preferred_element_type=F32)
        for index in range(4):
            begin = (2 * index + side) * frames
            out_ref[begin : begin + frames, :] = spread[:, index * LANES : index * LANES + lanes]
    which8 = lane_part((8, lanes))
    out_ref[8 * frames : 8 * frames + 8, :] = jnp.where(which8 == 0, centre[0], jnp.where(which8 == 1, centre[1], centre[2]))
    proj = packed_projection(is_first, gram_ref, out_ref, frames)
    proj_ref[...] = jnp.broadcast_to(proj[None], proj_ref.shape)


def lane_part(shape):
    lane = iota(shape, 1)
    third = shape[1] // 3
    return (lane >= third).astype(jnp.int32) + (lane >= 2 * third).astype(jnp.int32)


def fetch(refs, buffers, sems, others, chunks):
    width = refs[0].shape[2] // chunks
    copies = []
    for index, other in enumerate(others):
        for chunk in range(chunks):
            columns = pl.ds(chunk * width, width)
            group = []
            for which, (ref, buffer) in enumerate(zip(refs, buffers)):
                copy = pltpu.make_async_copy(
                    ref.at[other, :, columns], buffer.at[index, :, columns], sems.at[which, index * chunks + chunk]
                )
                copy.start()
                group.append(copy)
            copies.append(group)
    return copies


def copies_kernel(vec_ref, out_ref, sems):
    copies = [pltpu.make_async_copy(vec_ref, out_ref.at[index], sems.at[index]) for index in range(out_ref.shape[0])]
    for copy in copies:
        copy.start()
    for copy in copies:
        copy.wait()


def pass_kernel(core_ref, after_ref, out_ref):
    out_ref[0] = core_ref[0]


def gram_kernel(other, keep_hbm, recv_hbm, rows_ref, vec_ref, *rest):
    before, (out_ref, keep_ref, recv_ref, sems) = rest[:-4], rest[-4:]
    copies = fetch((keep_hbm, recv_hbm), (keep_ref, recv_ref), sems, (other,), sems.shape[1])
    total = before[0][...] if before else jnp.zeros(out_ref.shape, F32)
    chunks, pairs = len(copies), vec_ref.shape[0] // 2
    for pair in range(pairs):
        if pair % (pairs // chunks) == 0:
            for copy in copies[pair // (pairs // chunks)]:
                copy.wait()
        columns = slice(pair * PAIR, (pair + 1) * PAIR)
        left = jnp.concatenate([keep_ref[0, :, columns], recv_ref[0, :, columns], rows_ref[other, :, columns]], axis=0)
        right = jnp.concatenate([vec_ref[2 * pair], vec_ref[2 * pair + 1]], axis=1)
        total += lax.dot_general(left, right, NT, preferred_element_type=F32)
    out_ref[...] = total


def packed_projection(is_first, gram_ref, rot_ref, frames):
    lanes = gram_ref.shape[1]
    third = lanes // 3
    extra = gram_ref[6 * frames :, :]
    vec_sums = extra[9:10, :]
    centre = rot_ref[8 * frames : 8 * frames + 1, :]
    part = lane_part((1, lanes))
    along = [extra[i : i + 1] + extra[3 + i : 4 + i] + extra[6 + i : 7 + i] for i in range(3)]
    mean_term = jnp.where(part == 0, along[0], jnp.where(part == 1, along[1], along[2])) - centre * vec_sums
    halves = []
    for side in range(2):
        value = -rot_ref[(6 + side) * frames : (7 + side) * frames, :] * vec_sums - mean_term
        for j in range(3):
            spread = rot_ref[(2 * j + side) * frames : (2 * j + side + 1) * frames, :]
            begin = (3 * side + j) * frames
            value += spread * gram_ref[begin : begin + frames, :]
        halves.append(value)
    first = jnp.where(is_first, halves[0], halves[1])
    second = jnp.where(is_first, halves[1], halves[0])
    value = jnp.concatenate([first, second], axis=0)
    quarter = frames // 2
    row, col = iota((lanes, 4 * third), 0), iota((lanes, 4 * third), 1)
    packed = jnp.zeros((quarter, 4 * third), F32)
    pieces = split3(value)
    for q in range(4):
        fold = jnp.where((row % third == col % third) & (col // third == q), 1.0, 0.0).astype(BF16)
        for piece in pieces:
            packed += jnp.dot(piece[q * quarter : (q + 1) * quarter, :], fold, preferred_element_type=F32)
    return packed


def product_weights(is_first, parts_ref, rot_ref, weight_ref, frames, scale):
    lanes = rot_ref.shape[1]
    third = lanes // 3

    packed = parts_ref[0]
    for index in range(1, parts_ref.shape[0]):
        packed += parts_ref[index]
    packed = packed.astype(BF16)
    row, col = iota((4 * third, lanes), 0), iota((4 * third, lanes), 1)
    quarters = []
    for q in range(4):
        unfold = (row % third == col % third) & (row // third == q)
        quarters.append(jnp.dot(packed, unfold.astype(F32).astype(BF16), preferred_element_type=F32))
    first = jnp.concatenate(quarters[:2], axis=0)
    second = jnp.concatenate(quarters[2:], axis=0)
    sides = (jnp.where(is_first, first, second), jnp.where(is_first, second, first))
    centre = rot_ref[8 * frames : 8 * frames + 1, :]
    pieces = []
    proj_sum = jnp.zeros((1, lanes), F32)
    shift_sum = jnp.zeros((1, lanes), F32)
    for side in range(2):
        for j in range(3):
            begin = (2 * j + side) * frames
            pieces.append(rot_ref[begin : begin + frames, :] * sides[side])
        proj_sum += jnp.sum(sides[side], axis=0, keepdims=True)
        shift = rot_ref[(6 + side) * frames : (7 + side) * frames, :]
        shift_sum += jnp.sum(sides[side] * shift, axis=0, keepdims=True)
    at, part = iota((EXTRA, lanes), 0), lane_part((EXTRA, lanes))
    is_mean = (at < 9) & ((at == part) | (at == part + 3) | (at == part + 6))
    tail = jnp.where(is_mean, -proj_sum, jnp.where(at == 9, centre * proj_sum - shift_sum, 0.0))
    weight = jnp.concatenate(pieces + [tail], axis=0) * scale
    same = (iota((lanes, lanes), 0) == iota((lanes, lanes), 1)).astype(F32).astype(BF16)
    for index, piece in enumerate(split3(weight)):
        turned = lax.dot_general(same, piece, NT, preferred_element_type=F32)
        weight_ref[index * lanes : (index + 1) * lanes, :] = turned.astype(BF16)


def weighted(weight, refs, columns):
    term = jnp.dot(weight, jnp.concatenate([ref[0, :, columns] for ref in refs], axis=0), preferred_element_type=F32)
    lanes = term.shape[0] // 3
    return term[2 * lanes :] + term[lanes : 2 * lanes] + term[:lanes]


def product_kernel(
    scale, core_ref, parts_ref, rot_ref, keep_hbm, recv_hbm, rows_ref, up_ref, down_ref, weight_ref, keep_ref, recv_ref, sems
):
    chunks = sems.shape[1]
    copies = fetch((keep_hbm, recv_hbm), (keep_ref, recv_ref), sems, (1,), chunks)
    product_weights(core_ref[0] == 0, parts_ref, rot_ref, weight_ref, keep_ref.shape[1] // 3, scale)
    weight = weight_ref[...]
    pairs = up_ref.shape[0]
    for pair in range(pairs):
        if pair % (pairs // chunks) == 0:
            for copy in copies[pair // (pairs // chunks)]:
                copy.wait()
        columns = slice(pair * PAIR, (pair + 1) * PAIR)
        term = weighted(weight, (keep_ref, recv_ref, rows_ref.at[pl.ds(1, 1)]), columns).astype(BF16)
        out_ref = (up_ref, down_ref)[pair % 2]
        out_ref[pair // 2 * 2] = term[:, :LANES]
        out_ref[pair // 2 * 2 + 1] = term[:, LANES:]


def product_same_kernel(weight_ref, keep_ref, recv_ref, rows_ref, out_ref):
    weight = weight_ref[...]
    for pair in range(out_ref.shape[0] // 2):
        term = weighted(weight, (keep_ref, recv_ref, rows_ref), slice(pair * PAIR, (pair + 1) * PAIR))
        out_ref[2 * pair] = term[:, :LANES]
        out_ref[2 * pair + 1] = term[:, LANES:]


MIB = 1024 * 1024
GRAM_LIMIT = 16
GRAM_FLOPS = 1
ROTATION_FLOPS = 10**9
PASS_FLOPS = 40000000000
SMEM_SPEC = pl.BlockSpec(memory_space=pltpu.SMEM)


def params(limit=16):
    return pltpu.CompilerParams(vmem_limit_bytes=limit * MIB, dimension_semantics=("arbitrary",))


def cost(flops, moved):
    return pl.CostEstimate(flops=flops, bytes_accessed=moved, transcendentals=0)


def whole(*shape):
    return pl.BlockSpec(shape, lambda step: (0,) * len(shape))


def body(frames_xyz, mean_xyz, vector_block):
    frames, _, atoms = frames_xyz.shape
    kcount, _, own_atoms = vector_block.shape
    lanes = 3 * kcount
    rows = 3 * frames
    steps, quads = lax.axis_size("zh"), lax.axis_size("yh")
    chips = steps * quads
    peers = 2 * lax.axis_size("yl") * lax.axis_size("x")
    natom = atoms * lax.axis_size("yl") * lax.axis_size("x")
    frame_count = frames * 4 * chips
    ring = 2 * steps
    upward = [(i, (i + 1) % ring) for i in range(ring)]
    downward = [(i, (i - 1) % ring) for i in range(ring)]
    core = lax.axis_index("core").astype(jnp.int32).reshape(1)
    place = jnp.concatenate([lax.axis_index("zp").astype(jnp.int32).reshape(1), core])
    x_rows = frames_xyz.transpose(1, 0, 2).reshape(rows, atoms)
    vec_rows = vector_block.transpose(1, 0, 2).reshape(lanes, own_atoms)
    vmem, hbm = pl.BlockSpec(memory_space=pltpu.VMEM), pl.BlockSpec(memory_space=pl.ANY)
    limits = pltpu.CompilerParams(vmem_limit_bytes=16 * MIB)
    copies = pl.pallas_call(
        copies_kernel,
        in_specs=[hbm],
        out_specs=hbm,
        out_shape=jax.ShapeDtypeStruct((chips, lanes, own_atoms), BF16),
        scratch_shapes=[pltpu.SemaphoreType.DMA((chips,))],
        compiler_params=limits,
        cost_estimate=cost(1, 1),
        name="vector_copies",
    )(vec_rows)
    same = lax.all_to_all(copies, ("zh", "yh"), 0, 0, tiled=True)
    wide, narrow = atoms // steps, atoms // steps // 4
    both = lambda height: pl.BlockSpec((2, height, narrow), lambda step: (0, 0, step))
    part = lambda height, which: pl.BlockSpec((1, height, narrow), lambda step: (which, 0, step))
    sorted_shape = lambda height: jax.ShapeDtypeStruct((2, height, steps * narrow), BF16)
    keep, send, side, cross = pl.pallas_call(
        cross_kernel,
        grid=(steps,),
        in_specs=[
            SMEM_SPEC,
            pl.BlockSpec((rows, wide), lambda step: (0, step)),
            pl.BlockSpec((3, wide), lambda step: (0, step)),
        ],
        out_specs=[both(rows), both(rows), both(EXTRA), whole(peers, 8, rows + EXTRA)],
        out_shape=[
            sorted_shape(rows), sorted_shape(rows), sorted_shape(EXTRA), jax.ShapeDtypeStruct((peers, 8, rows + EXTRA), F32),
        ],
        scratch_shapes=[pltpu.VMEM((rows + EXTRA, EXTRA), F32)],
        compiler_params=params(),
        cost_estimate=cost(2 * rows * atoms * 256, 4 * rows * atoms),
        name="cross_terms",
    )(place, x_rows, mean_xyz)
    recv = lax.ppermute(send, "core", [(0, 1), (1, 0)])
    core_after = pl.pallas_call(
        pass_kernel,
        in_specs=[SMEM_SPEC, hbm],
        out_specs=SMEM_SPEC,
        out_shape=jax.ShapeDtypeStruct((1,), jnp.int32),
        cost_estimate=cost(PASS_FLOPS, 10**6),
        name="pass_core",
    )(core, cross)
    cross, core_after, same = lax.optimization_barrier((cross, core_after, same))
    opposite = lax.ppermute(same, ("zh", "zp"), downward)
    parts = lax.all_to_all(cross, ("core", "yl", "x"), 0, 0, tiled=True)
    blocks = lambda count: pl.BlockSpec((count, lanes, LANES), lambda step: (step, 0, 0))
    gram_rows = 2 * rows + EXTRA
    chunks = 2 if steps > 1 else 1
    fetched = [pltpu.VMEM((1, rows, steps * narrow), BF16)] * 2 + [pltpu.SemaphoreType.DMA((2, chunks))]
    def products(other, vec, *before):
        return pl.pallas_call(
            functools.partial(gram_kernel, other),
            in_specs=[hbm, hbm, vmem, vmem] + [vmem] * len(before),
            out_specs=vmem,
            out_shape=jax.ShapeDtypeStruct((gram_rows, lanes), F32),
            scratch_shapes=[
                *fetched,
            ],
            compiler_params=pltpu.CompilerParams(vmem_limit_bytes=GRAM_LIMIT * MIB),
            cost_estimate=cost(GRAM_FLOPS, 10**6),
            name="vector_products",
        )(keep, recv, side, vec, *before)

    gram = products(1, opposite, products(0, same))
    rot_shape = (8 * frames + 8, lanes)
    rot, proj = pl.pallas_call(
        functools.partial(rotation_kernel, natom),
        in_specs=[SMEM_SPEC, vmem, vmem],
        out_specs=[vmem, vmem],
        out_shape=[
            jax.ShapeDtypeStruct(rot_shape, F32),
            jax.ShapeDtypeStruct((peers, frames // 2, 4 * kcount), F32),
        ],
        compiler_params=limits,
        cost_estimate=cost(ROTATION_FLOPS, 10**6),
        name="rotation_projection",
    )(core_after, parts, gram)
    proj_parts = lax.all_to_all(proj, ("core", "yl", "x"), 0, 0, tiled=True)
    up, down, weight = pl.pallas_call(
        functools.partial(product_kernel, 1.0 / frame_count),
        in_specs=[SMEM_SPEC, vmem, vmem, hbm, hbm, vmem],
        out_specs=[vmem, vmem, vmem],
        out_shape=[
            jax.ShapeDtypeStruct((chips // 2, lanes, own_atoms), BF16),
            jax.ShapeDtypeStruct((chips // 2, lanes, own_atoms), BF16),
            jax.ShapeDtypeStruct((3 * lanes, gram_rows), BF16),
        ],
        scratch_shapes=fetched,
        compiler_params=limits,
        cost_estimate=cost(1, 1),
        name="product_terms",
    )(core, proj_parts, rot, keep, recv, side)
    shape = (chips // 2, lanes, own_atoms)
    from_below = lax.ppermute(up, ("zh", "zp"), upward)
    from_above = lax.ppermute(down, ("zh", "zp"), downward)
    own = pl.pallas_call(
        product_same_kernel,
        grid=(steps,),
        in_specs=[whole(3 * lanes, gram_rows), part(rows, 0), part(rows, 0), part(EXTRA, 0)],
        out_specs=blocks(quads),
        out_shape=jax.ShapeDtypeStruct((chips, lanes, LANES), F32),
        compiler_params=params(),
        cost_estimate=cost(2 * rows * atoms * 256, 4 * rows * atoms),
        name="product_terms_same",
    )(weight, keep, recv, side)
    halves = (steps, quads // 2, lanes, own_atoms)
    neighbours = jnp.concatenate([from_below.reshape(halves), from_above.reshape(halves)], axis=1)
    term = (own + neighbours.reshape(own.shape).astype(F32)).astype(BF16)
    terms = lax.all_to_all(term, ("zh", "yh"), 0, 0, tiled=True)
    total = jnp.sum(terms.astype(F32), axis=0)
    return total.reshape(3, kcount, own_atoms).transpose(1, 0, 2)


def solution(mesh):
    inner = Mesh(mesh.devices.reshape(mesh_sizes(mesh)), ("zh", "zp", "yh", "core", "yl", "x"))
    frames, coords = ("zh", "zp", "yh", "core"), ("yl", "x")
    in_specs = (P(frames, None, coords), P(None, coords), P(None, None, coords + frames))
    out_specs = P(None, None, coords + frames)
    return jax.shard_map(body, mesh=inner, in_specs=in_specs, out_specs=out_specs, check_vma=False)


def mesh_sizes(mesh):
    frames, coords = mesh.shape["frames"], mesh.shape["coords"]
    return (frames // 16, 2, 4, 2, 2, coords // 2)
```

```python
import functools

import jax
import jax.numpy as jnp
from jax import lax
from jax.experimental import pallas as pl
from jax.experimental.pallas import tpu as pltpu
from jax.sharding import Mesh
from jax.sharding import PartitionSpec as P

NS_STEPS = 8
LANES = 128
PAIR = 256
EXTRA = 16
F32 = jnp.float32
BF16 = jnp.bfloat16
HIGHEST = lax.Precision.HIGHEST
NT = (((1,), (1,)), ((), ()))
TN = (((0,), (0,)), ((), ()))


def iota(shape, dim):
    return lax.broadcasted_iota(jnp.int32, shape, dim)


def split3(value):
    high = value.astype(BF16)
    rest = value - high.astype(F32)
    middle = rest.astype(BF16)
    low = (rest - middle.astype(F32)).astype(BF16)
    return high, middle, low


def mean_rows(mean):
    shape = (EXTRA, mean.shape[1])
    row = iota(shape, 0)
    spread = jnp.where(row == 9, 1.0, 0.0)
    for i in range(3):
        spread = jnp.where((row < 9) & (row % 3 == i), mean[i : i + 1, :], spread)
    high, middle, low = split3(spread)
    take = jnp.where((row >= 3) & (row < 6), middle.astype(F32), jnp.where((row >= 6) & (row < 9), low.astype(F32), high.astype(F32)))
    return take.astype(BF16)


def cross_kernel(place_ref, x_ref, mean_ref, keep_ref, send_ref, rows_ref, cross_ref, acc_ref):
    step = pl.program_id(0)
    parity, core = place_ref[0], place_ref[1]
    extra = mean_rows(mean_ref[...])
    width = x_ref.shape[1]

    @pl.when(step == 0)
    def _():
        acc_ref[...] = jnp.zeros_like(acc_ref)

    total = acc_ref[...]
    pairs = width // PAIR
    for pair in range(pairs):
        columns = slice(pair * PAIR, (pair + 1) * PAIR)
        side = extra[:, columns]
        left = jnp.concatenate([x_ref[:, columns], side], axis=0)
        total += lax.dot_general(left, side, NT, preferred_element_type=F32)
        block = slice(pair % (pairs // 2) * LANES, (pair % (pairs // 2) + 1) * LANES)
        first, second = left[:, :LANES], left[:, LANES:]
        mine = jnp.where(core == 0, first, second)
        theirs = jnp.where(core == 0, second, first)
        other = (parity + pair // (pairs // 2)) % 2
        keep_ref[other, :, block] = mine[:-EXTRA]
        send_ref[other, :, block] = theirs[:-EXTRA]
        rows_ref[other, :, block] = mine[-EXTRA:]
    acc_ref[...] = total

    @pl.when(step == pl.num_programs(0) - 1)
    def _():
        row, col = iota((8, EXTRA), 0), iota((8, EXTRA), 1)
        pick = ((row < 3) & (col < 9) & ((col == row) | (col == row + 3) | (col == row + 6))) | ((row == 3) & (col == 9))
        cross = lax.dot_general(pick.astype(F32), total, NT, precision=HIGHEST, preferred_element_type=F32)
        cross_ref[...] = jnp.broadcast_to(cross[None], cross_ref.shape)


def polar_factor(amat):
    for _ in range(NS_STEPS):
        square = [[sum(amat[i][j] * amat[k][j] for j in range(3)) for k in range(3)] for i in range(3)]
        amat = [[1.5 * amat[i][j] - 0.5 * sum(square[i][k] * amat[k][j] for k in range(3)) for j in range(3)] for i in range(3)]
    return amat


def rotation_kernel(natom, core_ref, parts_ref, gram_ref, out_ref, proj_ref):
    half = parts_ref.shape[0] // 2
    frames = (parts_ref.shape[2] - EXTRA) // 3
    lanes = out_ref.shape[1]
    first, second = parts_ref[0], parts_ref[half]
    for index in range(1, half):
        first += parts_ref[index]
        second += parts_ref[half + index]
    is_first = core_ref[0] == 0
    own = jnp.where(is_first, first, second)
    other = jnp.where(is_first, second, first)
    ones_at = 3 * frames + 9
    centre = [own[i : i + 1, ones_at : ones_at + 1] / natom for i in range(3)]
    columns = [[total[:, j * frames : (j + 1) * frames] for total in (own, other)] for j in range(3)]
    row = lambda index, j: jnp.concatenate([part[index : index + 1] for part in columns[j]], axis=0)
    sums = [row(3, j) for j in range(3)]
    cross = [[row(i, j) - centre[i] * sums[j] for j in range(3)] for i in range(3)]
    scale = jnp.sqrt(1.0 + sum(cross[i][j] * cross[i][j] for i in range(3) for j in range(3)))
    rotation = polar_factor([[cross[i][j] / scale for j in range(3)] for i in range(3)])
    shift = [sum(rotation[i][j] * (sums[j] / natom) for j in range(3)) for i in range(3)]
    entries = [rotation[i][j] for i in range(3) for j in range(3)] + shift
    at = iota((EXTRA, frames), 0)
    index3, lane = iota((3 * EXTRA, 4 * LANES), 0) % EXTRA, iota((3 * EXTRA, 4 * LANES), 1)
    third = lanes // 3
    place, within = lane // LANES, lane % LANES
    which = within // third
    chosen = ((place < 3) & (index3 == 3 * which + place)) | ((place == 3) & (index3 == 9 + which))
    chosen = jnp.where(chosen & (which < 3), 1.0, 0.0).astype(BF16)
    for side in range(2):
        packed = jnp.zeros((EXTRA, frames), F32)
        for index, entry in enumerate(entries):
            packed = jnp.where(at == index, entry[side : side + 1], packed)
        pieces = jnp.concatenate([piece.astype(F32) for piece in split3(packed)], axis=0).astype(BF16)
        spread = lax.dot_general(pieces, chosen, TN, preferred_element_type=F32)
        for index in range(4):
            begin = (2 * index + side) * frames
            out_ref[begin : begin + frames, :] = spread[:, index * LANES : index * LANES + lanes]
    which8 = lane_part((8, lanes))
    out_ref[8 * frames : 8 * frames + 8, :] = jnp.where(which8 == 0, centre[0], jnp.where(which8 == 1, centre[1], centre[2]))
    proj = packed_projection(is_first, gram_ref, out_ref, frames)
    proj_ref[...] = jnp.broadcast_to(proj.astype(BF16)[None], proj_ref.shape)


def lane_part(shape):
    lane = iota(shape, 1)
    third = shape[1] // 3
    return (lane >= third).astype(jnp.int32) + (lane >= 2 * third).astype(jnp.int32)


def fetch(refs, buffers, sems, others, chunks):
    width = refs[0].shape[2] // chunks
    copies = []
    for index, other in enumerate(others):
        for chunk in range(chunks):
            columns = pl.ds(chunk * width, width)
            group = []
            for which, (ref, buffer) in enumerate(zip(refs, buffers)):
                copy = pltpu.make_async_copy(
                    ref.at[other, :, columns], buffer.at[index, :, columns], sems.at[which, index * chunks + chunk]
                )
                copy.start()
                group.append(copy)
            copies.append(group)
    return copies


def copies_kernel(vec_ref, out_ref, sems):
    copies = [pltpu.make_async_copy(vec_ref, out_ref.at[index], sems.at[index]) for index in range(out_ref.shape[0])]
    for copy in copies:
        copy.start()
    for copy in copies:
        copy.wait()


def pass_kernel(core_ref, after_ref, out_ref):
    out_ref[0] = core_ref[0]


def by_yh(at, quads, pairs):
    return at % quads * (2 * pairs // quads) + at // quads


def gram_kernel(quads, other, keep_hbm, recv_hbm, rows_ref, vec_ref, *rest):
    before, (out_ref, keep_ref, recv_ref, sems) = rest[:-4], rest[-4:]
    copies = fetch((keep_hbm, recv_hbm), (keep_ref, recv_ref), sems, (other,), sems.shape[1])
    total = before[0][...] if before else jnp.zeros(out_ref.shape, F32)
    chunks, pairs = len(copies), vec_ref.shape[0] // 2
    for pair in range(pairs):
        if pair % (pairs // chunks) == 0:
            for copy in copies[pair // (pairs // chunks)]:
                copy.wait()
        columns = slice(pair * PAIR, (pair + 1) * PAIR)
        left = jnp.concatenate([keep_ref[0, :, columns], recv_ref[0, :, columns], rows_ref[other, :, columns]], axis=0)
        right = jnp.concatenate([vec_ref[by_yh(at, quads, pairs)] for at in (2 * pair, 2 * pair + 1)], axis=1)
        total += lax.dot_general(left, right, NT, preferred_element_type=F32)
    out_ref[...] = total


def packed_projection(is_first, gram_ref, rot_ref, frames):
    lanes = gram_ref.shape[1]
    third = lanes // 3
    extra = gram_ref[6 * frames :, :]
    vec_sums = extra[9:10, :]
    centre = rot_ref[8 * frames : 8 * frames + 1, :]
    part = lane_part((1, lanes))
    along = [extra[i : i + 1] + extra[3 + i : 4 + i] + extra[6 + i : 7 + i] for i in range(3)]
    mean_term = jnp.where(part == 0, along[0], jnp.where(part == 1, along[1], along[2])) - centre * vec_sums
    halves = []
    for side in range(2):
        value = -rot_ref[(6 + side) * frames : (7 + side) * frames, :] * vec_sums - mean_term
        for j in range(3):
            spread = rot_ref[(2 * j + side) * frames : (2 * j + side + 1) * frames, :]
            begin = (3 * side + j) * frames
            value += spread * gram_ref[begin : begin + frames, :]
        halves.append(value)
    first = jnp.where(is_first, halves[0], halves[1])
    second = jnp.where(is_first, halves[1], halves[0])
    value = jnp.concatenate([first, second], axis=0)
    quarter = frames // 2
    row, col = iota((lanes, 4 * third), 0), iota((lanes, 4 * third), 1)
    packed = jnp.zeros((quarter, 4 * third), F32)
    pieces = split3(value)
    for q in range(4):
        fold = jnp.where((row % third == col % third) & (col // third == q), 1.0, 0.0).astype(BF16)
        for piece in pieces:
            packed += jnp.dot(piece[q * quarter : (q + 1) * quarter, :], fold, preferred_element_type=F32)
    return packed


def product_weights(is_first, parts_ref, rot_ref, weight_ref, frames, scale):
    lanes = rot_ref.shape[1]
    third = lanes // 3

    packed = parts_ref[0].astype(F32)
    for index in range(1, parts_ref.shape[0]):
        packed += parts_ref[index].astype(F32)
    packed = packed.astype(BF16)
    row, col = iota((4 * third, lanes), 0), iota((4 * third, lanes), 1)
    quarters = []
    for q in range(4):
        unfold = (row % third == col % third) & (row // third == q)
        quarters.append(jnp.dot(packed, unfold.astype(F32).astype(BF16), preferred_element_type=F32))
    first = jnp.concatenate(quarters[:2], axis=0)
    second = jnp.concatenate(quarters[2:], axis=0)
    sides = (jnp.where(is_first, first, second), jnp.where(is_first, second, first))
    centre = rot_ref[8 * frames : 8 * frames + 1, :]
    pieces = []
    proj_sum = jnp.zeros((1, lanes), F32)
    shift_sum = jnp.zeros((1, lanes), F32)
    for side in range(2):
        for j in range(3):
            begin = (2 * j + side) * frames
            pieces.append(rot_ref[begin : begin + frames, :] * sides[side])
        proj_sum += jnp.sum(sides[side], axis=0, keepdims=True)
        shift = rot_ref[(6 + side) * frames : (7 + side) * frames, :]
        shift_sum += jnp.sum(sides[side] * shift, axis=0, keepdims=True)
    at, part = iota((EXTRA, lanes), 0), lane_part((EXTRA, lanes))
    is_mean = (at < 9) & ((at == part) | (at == part + 3) | (at == part + 6))
    tail = jnp.where(is_mean, -proj_sum, jnp.where(at == 9, centre * proj_sum - shift_sum, 0.0))
    weight = jnp.concatenate(pieces + [tail], axis=0) * scale
    same = (iota((lanes, lanes), 0) == iota((lanes, lanes), 1)).astype(F32).astype(BF16)
    for index, piece in enumerate(split3(weight)):
        turned = lax.dot_general(same, piece, NT, preferred_element_type=F32)
        weight_ref[index * lanes : (index + 1) * lanes, :] = turned.astype(BF16)


def weighted(weight, refs, columns):
    term = jnp.dot(weight, jnp.concatenate([ref[0, :, columns] for ref in refs], axis=0), preferred_element_type=F32)
    lanes = term.shape[0] // 3
    return term[2 * lanes :] + term[lanes : 2 * lanes] + term[:lanes]


def product_kernel(
    scale, quads, core_ref, parts_ref, rot_ref, keep_hbm, recv_hbm, rows_ref, up_ref, down_ref, weight_ref, keep_ref, recv_ref, sems
):
    chunks = sems.shape[1]
    copies = fetch((keep_hbm, recv_hbm), (keep_ref, recv_ref), sems, (1,), chunks)
    product_weights(core_ref[0] == 0, parts_ref, rot_ref, weight_ref, keep_ref.shape[1] // 3, scale)
    weight = weight_ref[...]
    pairs = up_ref.shape[0]
    for pair in range(pairs):
        if pair % (pairs // chunks) == 0:
            for copy in copies[pair // (pairs // chunks)]:
                copy.wait()
        columns = slice(pair * PAIR, (pair + 1) * PAIR)
        term = weighted(weight, (keep_ref, recv_ref, rows_ref.at[pl.ds(1, 1)]), columns).astype(BF16)
        for index in range(2):
            at = by_yh(2 * pair + index, quads, pairs)
            (up_ref if at < pairs else down_ref)[at % pairs] = term[:, index * LANES : (index + 1) * LANES]


def product_same_kernel(weight_ref, keep_ref, recv_ref, rows_ref, out_ref):
    weight = weight_ref[...]
    for pair in range(out_ref.shape[0] // 2):
        term = weighted(weight, (keep_ref, recv_ref, rows_ref), slice(pair * PAIR, (pair + 1) * PAIR))
        out_ref[2 * pair, 0] = term[:, :LANES]
        out_ref[2 * pair + 1, 0] = term[:, LANES:]


MIB = 1024 * 1024
GRAM_LIMIT = 16
GRAM_FLOPS = 1
ROTATION_FLOPS = 10**9
PASS_FLOPS = 40000000000
SMEM_SPEC = pl.BlockSpec(memory_space=pltpu.SMEM)


def params(limit=16):
    return pltpu.CompilerParams(vmem_limit_bytes=limit * MIB, dimension_semantics=("arbitrary",))


def cost(flops, moved):
    return pl.CostEstimate(flops=flops, bytes_accessed=moved, transcendentals=0)


def whole(*shape):
    return pl.BlockSpec(shape, lambda step: (0,) * len(shape))


def body(frames_xyz, mean_xyz, vector_block):
    frames, _, atoms = frames_xyz.shape
    kcount, _, own_atoms = vector_block.shape
    lanes = 3 * kcount
    rows = 3 * frames
    steps, quads = lax.axis_size("zh"), lax.axis_size("yh")
    chips = steps * quads
    peers = 2 * lax.axis_size("yl") * lax.axis_size("x")
    natom = atoms * lax.axis_size("yl") * lax.axis_size("x")
    frame_count = frames * 4 * chips
    ring = 2 * steps
    upward = [(i, (i + 1) % ring) for i in range(ring)]
    downward = [(i, (i - 1) % ring) for i in range(ring)]
    core = lax.axis_index("core").astype(jnp.int32).reshape(1)
    place = jnp.concatenate([lax.axis_index("zp").astype(jnp.int32).reshape(1), core])
    x_rows = frames_xyz.transpose(1, 0, 2).reshape(rows, atoms)
    vec_rows = vector_block.transpose(1, 0, 2).reshape(lanes, own_atoms)
    vmem, hbm = pl.BlockSpec(memory_space=pltpu.VMEM), pl.BlockSpec(memory_space=pl.ANY)
    limits = pltpu.CompilerParams(vmem_limit_bytes=16 * MIB)
    copies = pl.pallas_call(
        copies_kernel,
        in_specs=[hbm],
        out_specs=hbm,
        out_shape=jax.ShapeDtypeStruct((chips, lanes, own_atoms), BF16),
        scratch_shapes=[pltpu.SemaphoreType.DMA((chips,))],
        compiler_params=limits,
        cost_estimate=cost(1, 1),
        name="vector_copies",
    )(vec_rows)
    same = lax.all_to_all(copies, ("yh", "zh"), 0, 0, tiled=True)
    wide, narrow = atoms // steps, atoms // steps // 4
    both = lambda height: pl.BlockSpec((2, height, narrow), lambda step: (0, 0, step))
    part = lambda height, which: pl.BlockSpec((1, height, narrow), lambda step: (which, 0, step))
    sorted_shape = lambda height: jax.ShapeDtypeStruct((2, height, steps * narrow), BF16)
    keep, send, side, cross = pl.pallas_call(
        cross_kernel,
        grid=(steps,),
        in_specs=[
            SMEM_SPEC,
            pl.BlockSpec((rows, wide), lambda step: (0, step)),
            pl.BlockSpec((3, wide), lambda step: (0, step)),
        ],
        out_specs=[both(rows), both(rows), both(EXTRA), whole(peers, 8, rows + EXTRA)],
        out_shape=[
            sorted_shape(rows), sorted_shape(rows), sorted_shape(EXTRA), jax.ShapeDtypeStruct((peers, 8, rows + EXTRA), F32),
        ],
        scratch_shapes=[pltpu.VMEM((rows + EXTRA, EXTRA), F32)],
        compiler_params=params(),
        cost_estimate=cost(2 * rows * atoms * 256, 4 * rows * atoms),
        name="cross_terms",
    )(place, x_rows, mean_xyz)
    recv = lax.ppermute(send, "core", [(0, 1), (1, 0)])
    core_after = pl.pallas_call(
        pass_kernel,
        in_specs=[SMEM_SPEC, hbm],
        out_specs=SMEM_SPEC,
        out_shape=jax.ShapeDtypeStruct((1,), jnp.int32),
        cost_estimate=cost(PASS_FLOPS, 10**6),
        name="pass_core",
    )(core, cross)
    cross, core_after, same = lax.optimization_barrier((cross, core_after, same))
    opposite = lax.ppermute(same, ("zh", "zp"), downward)
    parts = lax.all_to_all(cross, ("core", "yl", "x"), 0, 0, tiled=True)
    blocks = lambda count: pl.BlockSpec((count, lanes, LANES), lambda step: (step, 0, 0))
    gram_rows = 2 * rows + EXTRA
    chunks = 2 if steps > 1 else 1
    fetched = [pltpu.VMEM((1, rows, steps * narrow), BF16)] * 2 + [pltpu.SemaphoreType.DMA((2, chunks))]
    def products(other, vec, *before):
        return pl.pallas_call(
            functools.partial(gram_kernel, quads, other),
            in_specs=[hbm, hbm, vmem, vmem] + [vmem] * len(before),
            out_specs=vmem,
            out_shape=jax.ShapeDtypeStruct((gram_rows, lanes), F32),
            scratch_shapes=[
                *fetched,
            ],
            compiler_params=pltpu.CompilerParams(vmem_limit_bytes=GRAM_LIMIT * MIB),
            cost_estimate=cost(GRAM_FLOPS, 10**6),
            name="vector_products",
        )(keep, recv, side, vec, *before)

    gram = products(1, opposite, products(0, same))
    rot_shape = (8 * frames + 8, lanes)
    rot, proj = pl.pallas_call(
        functools.partial(rotation_kernel, natom),
        in_specs=[SMEM_SPEC, vmem, vmem],
        out_specs=[vmem, vmem],
        out_shape=[
            jax.ShapeDtypeStruct(rot_shape, F32),
            jax.ShapeDtypeStruct((peers, frames // 2, 4 * kcount), BF16),
        ],
        compiler_params=limits,
        cost_estimate=cost(ROTATION_FLOPS, 10**6),
        name="rotation_projection",
    )(core_after, parts, gram)
    proj_parts = lax.all_to_all(proj, ("core", "yl", "x"), 0, 0, tiled=True)
    up, down, weight = pl.pallas_call(
        functools.partial(product_kernel, 1.0 / frame_count, quads),
        in_specs=[SMEM_SPEC, vmem, vmem, hbm, hbm, vmem],
        out_specs=[vmem, vmem, vmem],
        out_shape=[
            jax.ShapeDtypeStruct((chips // 2, lanes, own_atoms), BF16),
            jax.ShapeDtypeStruct((chips // 2, lanes, own_atoms), BF16),
            jax.ShapeDtypeStruct((3 * lanes, gram_rows), BF16),
        ],
        scratch_shapes=fetched,
        compiler_params=limits,
        cost_estimate=cost(1, 1),
        name="product_terms",
    )(core, proj_parts, rot, keep, recv, side)
    shape = (chips // 2, lanes, own_atoms)
    from_below = lax.ppermute(up, ("zh", "zp"), upward)
    from_above = lax.ppermute(down, ("zh", "zp"), downward)
    own = pl.pallas_call(
        product_same_kernel,
        grid=(steps,),
        in_specs=[whole(3 * lanes, gram_rows), part(rows, 0), part(rows, 0), part(EXTRA, 0)],
        out_specs=pl.BlockSpec((quads, 1, lanes, LANES), lambda step: (0, step, 0, 0)),
        out_shape=jax.ShapeDtypeStruct((quads, steps, lanes, LANES), F32),
        compiler_params=params(),
        cost_estimate=cost(2 * rows * atoms * 256, 4 * rows * atoms),
        name="product_terms_same",
    )(weight, keep, recv, side)
    neighbours = jnp.concatenate([from_below, from_above], axis=0)
    term = (own.reshape(neighbours.shape) + neighbours.astype(F32)).astype(BF16)
    terms = lax.all_to_all(term, ("yh", "zh"), 0, 0, tiled=True)
    total = jnp.sum(terms.astype(F32), axis=0)
    return total.reshape(3, kcount, own_atoms).transpose(1, 0, 2)


def solution(mesh):
    inner = Mesh(mesh.devices.reshape(mesh_sizes(mesh)), ("zh", "zp", "yh", "core", "yl", "x"))
    frames, coords = ("zh", "zp", "yh", "core"), ("yl", "x")
    in_specs = (P(frames, None, coords), P(None, coords), P(None, None, coords + frames))
    out_specs = P(None, None, coords + frames)
    return jax.shard_map(body, mesh=inner, in_specs=in_specs, out_specs=out_specs, check_vma=False)


def mesh_sizes(mesh):
    frames, coords = mesh.shape["frames"], mesh.shape["coords"]
    return (frames // 16, 2, 4, 2, 2, coords // 2)
```

```python
import functools

import jax
import jax.numpy as jnp
from jax import lax
from jax.experimental import pallas as pl
from jax.experimental.pallas import tpu as pltpu
from jax.sharding import Mesh
from jax.sharding import PartitionSpec as P

NS_STEPS = 8
LANES = 128
PAIR = 256
EXTRA = 16
F32 = jnp.float32
BF16 = jnp.bfloat16
HIGHEST = lax.Precision.HIGHEST
NT = (((1,), (1,)), ((), ()))
TN = (((0,), (0,)), ((), ()))


def iota(shape, dim):
    return lax.broadcasted_iota(jnp.int32, shape, dim)


def split3(value):
    high = value.astype(BF16)
    rest = value - high.astype(F32)
    middle = rest.astype(BF16)
    low = (rest - middle.astype(F32)).astype(BF16)
    return high, middle, low


def mean_rows(mean):
    shape = (EXTRA, mean.shape[1])
    row = iota(shape, 0)
    spread = jnp.where(row == 9, 1.0, 0.0)
    for i in range(3):
        spread = jnp.where((row < 9) & (row % 3 == i), mean[i : i + 1, :], spread)
    high, middle, low = split3(spread)
    take = jnp.where((row >= 3) & (row < 6), middle.astype(F32), jnp.where((row >= 6) & (row < 9), low.astype(F32), high.astype(F32)))
    return take.astype(BF16)


def cross_kernel(place_ref, x_ref, mean_ref, keep_ref, send_ref, rows_ref, cross_ref, acc_ref):
    step = pl.program_id(0)
    parity, core = place_ref[0], place_ref[1]
    extra = mean_rows(mean_ref[...])
    width = x_ref.shape[1]

    @pl.when(step == 0)
    def _():
        acc_ref[...] = jnp.zeros_like(acc_ref)

    total = acc_ref[...]
    pairs = width // PAIR
    for pair in range(pairs):
        columns = slice(pair * PAIR, (pair + 1) * PAIR)
        side = extra[:, columns]
        left = jnp.concatenate([x_ref[:, columns], side], axis=0)
        total += lax.dot_general(left, side, NT, preferred_element_type=F32)
        block = slice(pair % (pairs // 2) * LANES, (pair % (pairs // 2) + 1) * LANES)
        first, second = left[:, :LANES], left[:, LANES:]
        mine = jnp.where(core == 0, first, second)
        theirs = jnp.where(core == 0, second, first)
        other = (parity + pair // (pairs // 2)) % 2
        keep_ref[other, :, block] = mine[:-EXTRA]
        send_ref[other, :, block] = theirs[:-EXTRA]
        rows_ref[other, :, block] = mine[-EXTRA:]
    acc_ref[...] = total

    @pl.when(step == pl.num_programs(0) - 1)
    def _():
        row, col = iota((8, EXTRA), 0), iota((8, EXTRA), 1)
        pick = ((row < 3) & (col < 9) & ((col == row) | (col == row + 3) | (col == row + 6))) | ((row == 3) & (col == 9))
        cross = lax.dot_general(pick.astype(F32), total, NT, precision=HIGHEST, preferred_element_type=F32)
        cross_ref[...] = jnp.broadcast_to(cross[None], cross_ref.shape)


def polar_factor(amat):
    for _ in range(NS_STEPS):
        square = [[sum(amat[i][j] * amat[k][j] for j in range(3)) for k in range(3)] for i in range(3)]
        amat = [[1.5 * amat[i][j] - 0.5 * sum(square[i][k] * amat[k][j] for k in range(3)) for j in range(3)] for i in range(3)]
    return amat


def rotation_kernel(natom, core_ref, parts_ref, gram_ref, out_ref, proj_ref):
    half = parts_ref.shape[0] // 2
    frames = (parts_ref.shape[2] - EXTRA) // 3
    lanes = out_ref.shape[1]
    first, second = parts_ref[0], parts_ref[half]
    for index in range(1, half):
        first += parts_ref[index]
        second += parts_ref[half + index]
    is_first = core_ref[0] == 0
    own = jnp.where(is_first, first, second)
    other = jnp.where(is_first, second, first)
    ones_at = 3 * frames + 9
    centre = [own[i : i + 1, ones_at : ones_at + 1] / natom for i in range(3)]
    columns = [[total[:, j * frames : (j + 1) * frames] for total in (own, other)] for j in range(3)]
    row = lambda index, j: jnp.concatenate([part[index : index + 1] for part in columns[j]], axis=0)
    sums = [row(3, j) for j in range(3)]
    cross = [[row(i, j) - centre[i] * sums[j] for j in range(3)] for i in range(3)]
    scale = jnp.sqrt(1.0 + sum(cross[i][j] * cross[i][j] for i in range(3) for j in range(3)))
    rotation = polar_factor([[cross[i][j] / scale for j in range(3)] for i in range(3)])
    shift = [sum(rotation[i][j] * (sums[j] / natom) for j in range(3)) for i in range(3)]
    entries = [rotation[i][j] for i in range(3) for j in range(3)] + shift
    at = iota((EXTRA, frames), 0)
    index3, lane = iota((3 * EXTRA, 4 * LANES), 0) % EXTRA, iota((3 * EXTRA, 4 * LANES), 1)
    third = lanes // 3
    place, within = lane // LANES, lane % LANES
    which = within // third
    chosen = ((place < 3) & (index3 == 3 * which + place)) | ((place == 3) & (index3 == 9 + which))
    chosen = jnp.where(chosen & (which < 3), 1.0, 0.0).astype(BF16)
    for side in range(2):
        packed = jnp.zeros((EXTRA, frames), F32)
        for index, entry in enumerate(entries):
            packed = jnp.where(at == index, entry[side : side + 1], packed)
        pieces = jnp.concatenate([piece.astype(F32) for piece in split3(packed)], axis=0).astype(BF16)
        spread = lax.dot_general(pieces, chosen, TN, preferred_element_type=F32)
        for index in range(4):
            begin = (2 * index + side) * frames
            out_ref[begin : begin + frames, :] = spread[:, index * LANES : index * LANES + lanes]
    which8 = lane_part((8, lanes))
    out_ref[8 * frames : 8 * frames + 8, :] = jnp.where(which8 == 0, centre[0], jnp.where(which8 == 1, centre[1], centre[2]))
    proj = packed_projection(is_first, gram_ref, out_ref, frames)
    proj_ref[...] = jnp.broadcast_to(proj.astype(BF16)[None], proj_ref.shape)


def lane_part(shape):
    lane = iota(shape, 1)
    third = shape[1] // 3
    return (lane >= third).astype(jnp.int32) + (lane >= 2 * third).astype(jnp.int32)


def fetch(refs, buffers, sems, others, chunks):
    width = refs[0].shape[2] // chunks
    copies = []
    for index, other in enumerate(others):
        for chunk in range(chunks):
            columns = pl.ds(chunk * width, width)
            group = []
            for which, (ref, buffer) in enumerate(zip(refs, buffers)):
                copy = pltpu.make_async_copy(
                    ref.at[other, :, columns], buffer.at[index, :, columns], sems.at[which, index * chunks + chunk]
                )
                copy.start()
                group.append(copy)
            copies.append(group)
    return copies


def copies_kernel(vec_ref, out_ref, sems):
    copies = [pltpu.make_async_copy(vec_ref, out_ref.at[index], sems.at[index]) for index in range(out_ref.shape[0])]
    for copy in copies:
        copy.start()
    for copy in copies:
        copy.wait()


def pass_kernel(core_ref, after_ref, out_ref):
    out_ref[0] = core_ref[0]


def by_yh(at, quads, pairs):
    return at % quads * (2 * pairs // quads) + at // quads


def gram_kernel(quads, other, keep_hbm, recv_hbm, rows_ref, vec_ref, *rest):
    before, (out_ref, keep_ref, recv_ref, sems) = rest[:-4], rest[-4:]
    copies = fetch((keep_hbm, recv_hbm), (keep_ref, recv_ref), sems, (other,), sems.shape[1])
    total = before[0][...] if before else jnp.zeros(out_ref.shape, F32)
    chunks, pairs = len(copies), vec_ref.shape[0] // 2
    for pair in range(pairs):
        if pair % (pairs // chunks) == 0:
            for copy in copies[pair // (pairs // chunks)]:
                copy.wait()
        columns = slice(pair * PAIR, (pair + 1) * PAIR)
        left = jnp.concatenate([keep_ref[0, :, columns], recv_ref[0, :, columns], rows_ref[other, :, columns]], axis=0)
        right = jnp.concatenate([vec_ref[by_yh(at, quads, pairs)] for at in (2 * pair, 2 * pair + 1)], axis=1)
        total += lax.dot_general(left, right, NT, preferred_element_type=F32)
    out_ref[...] = total


def packed_projection(is_first, gram_ref, rot_ref, frames):
    lanes = gram_ref.shape[1]
    third = lanes // 3
    extra = gram_ref[6 * frames :, :]
    vec_sums = extra[9:10, :]
    centre = rot_ref[8 * frames : 8 * frames + 1, :]
    part = lane_part((1, lanes))
    along = [extra[i : i + 1] + extra[3 + i : 4 + i] + extra[6 + i : 7 + i] for i in range(3)]
    mean_term = jnp.where(part == 0, along[0], jnp.where(part == 1, along[1], along[2])) - centre * vec_sums
    halves = []
    for side in range(2):
        value = -rot_ref[(6 + side) * frames : (7 + side) * frames, :] * vec_sums - mean_term
        for j in range(3):
            spread = rot_ref[(2 * j + side) * frames : (2 * j + side + 1) * frames, :]
            begin = (3 * side + j) * frames
            value += spread * gram_ref[begin : begin + frames, :]
        halves.append(value)
    first = jnp.where(is_first, halves[0], halves[1])
    second = jnp.where(is_first, halves[1], halves[0])
    value = jnp.concatenate([first, second], axis=0)
    quarter = frames // 2
    row, col = iota((lanes, 4 * third), 0), iota((lanes, 4 * third), 1)
    packed = jnp.zeros((quarter, 4 * third), F32)
    pieces = split3(value)
    for q in range(4):
        fold = jnp.where((row % third == col % third) & (col // third == q), 1.0, 0.0).astype(BF16)
        for piece in pieces:
            packed += jnp.dot(piece[q * quarter : (q + 1) * quarter, :], fold, preferred_element_type=F32)
    return packed


def product_weights(is_first, parts_ref, rot_ref, weight_ref, frames, scale):
    lanes = rot_ref.shape[1]
    third = lanes // 3

    packed = parts_ref[0].astype(F32)
    for index in range(1, parts_ref.shape[0]):
        packed += parts_ref[index].astype(F32)
    packed = packed.astype(BF16)
    row, col = iota((4 * third, lanes), 0), iota((4 * third, lanes), 1)
    quarters = []
    for q in range(4):
        unfold = (row % third == col % third) & (row // third == q)
        quarters.append(jnp.dot(packed, unfold.astype(F32).astype(BF16), preferred_element_type=F32))
    first = jnp.concatenate(quarters[:2], axis=0)
    second = jnp.concatenate(quarters[2:], axis=0)
    sides = (jnp.where(is_first, first, second), jnp.where(is_first, second, first))
    centre = rot_ref[8 * frames : 8 * frames + 1, :]
    pieces = []
    proj_sum = jnp.zeros((1, lanes), F32)
    shift_sum = jnp.zeros((1, lanes), F32)
    for side in range(2):
        for j in range(3):
            begin = (2 * j + side) * frames
            pieces.append(rot_ref[begin : begin + frames, :] * sides[side])
        proj_sum += jnp.sum(sides[side], axis=0, keepdims=True)
        shift = rot_ref[(6 + side) * frames : (7 + side) * frames, :]
        shift_sum += jnp.sum(sides[side] * shift, axis=0, keepdims=True)
    at, part = iota((EXTRA, lanes), 0), lane_part((EXTRA, lanes))
    is_mean = (at < 9) & ((at == part) | (at == part + 3) | (at == part + 6))
    tail = jnp.where(is_mean, -proj_sum, jnp.where(at == 9, centre * proj_sum - shift_sum, 0.0))
    weight = jnp.concatenate(pieces + [tail], axis=0) * scale
    same = (iota((lanes, lanes), 0) == iota((lanes, lanes), 1)).astype(F32).astype(BF16)
    for index, piece in enumerate(split3(weight)):
        turned = lax.dot_general(same, piece, NT, preferred_element_type=F32)
        weight_ref[index * lanes : (index + 1) * lanes, :] = turned.astype(BF16)


def weighted(weight, refs, columns):
    term = jnp.dot(weight, jnp.concatenate([ref[0, :, columns] for ref in refs], axis=0), preferred_element_type=F32)
    lanes = term.shape[0] // 3
    return term[2 * lanes :] + term[lanes : 2 * lanes] + term[:lanes]


def product_kernel(
    scale, quads, core_ref, parts_ref, rot_ref, keep_hbm, recv_hbm, rows_ref, up_ref, down_ref, weight_ref, keep_ref, recv_ref, sems
):
    chunks = sems.shape[1]
    copies = fetch((keep_hbm, recv_hbm), (keep_ref, recv_ref), sems, (1,), chunks)
    product_weights(core_ref[0] == 0, parts_ref, rot_ref, weight_ref, keep_ref.shape[1] // 3, scale)
    weight = weight_ref[...]
    pairs = (up_ref.shape[0] + down_ref.shape[0]) // 2
    for pair in range(pairs):
        if pair % (pairs // chunks) == 0:
            for copy in copies[pair // (pairs // chunks)]:
                copy.wait()
        columns = slice(pair * PAIR, (pair + 1) * PAIR)
        term = weighted(weight, (keep_ref, recv_ref, rows_ref.at[pl.ds(1, 1)]), columns).astype(BF16)
        for index in range(2):
            at = by_yh(2 * pair + index, quads, pairs)
            ref, at = (up_ref, at) if at < up_ref.shape[0] else (down_ref, at - up_ref.shape[0])
            ref[at] = term[:, index * LANES : (index + 1) * LANES]


def product_same_kernel(weight_ref, keep_hbm, recv_hbm, rows_ref, out_ref, keep_ref, recv_ref, sems):
    chunks = sems.shape[1]
    copies = fetch((keep_hbm, recv_hbm), (keep_ref, recv_ref), sems, (0,), chunks)
    weight = weight_ref[...]
    quads = out_ref.shape[0]
    pairs = quads * out_ref.shape[1] // 2
    for pair in range(pairs):
        if pair % (pairs // chunks) == 0:
            for copy in copies[pair // (pairs // chunks)]:
                copy.wait()
        columns = slice(pair * PAIR, (pair + 1) * PAIR)
        term = weighted(weight, (keep_ref, recv_ref, rows_ref.at[pl.ds(0, 1)]), columns)
        for index in range(2):
            high, quad = divmod(2 * pair + index, quads)
            out_ref[quad, high] = term[:, index * LANES : (index + 1) * LANES]


MIB = 1024 * 1024
UP_SHARE = 10
GRAM_LIMIT = 16
GRAM_FLOPS = 1
ROTATION_FLOPS = 10**9
PASS_FLOPS = 40000000000
SMEM_SPEC = pl.BlockSpec(memory_space=pltpu.SMEM)


def params(limit=16):
    return pltpu.CompilerParams(vmem_limit_bytes=limit * MIB, dimension_semantics=("arbitrary",))


def cost(flops, moved):
    return pl.CostEstimate(flops=flops, bytes_accessed=moved, transcendentals=0)


def whole(*shape):
    return pl.BlockSpec(shape, lambda step: (0,) * len(shape))


def body(frames_xyz, mean_xyz, vector_block):
    frames, _, atoms = frames_xyz.shape
    kcount, _, own_atoms = vector_block.shape
    lanes = 3 * kcount
    rows = 3 * frames
    steps, quads = lax.axis_size("zh"), lax.axis_size("yh")
    chips = steps * quads
    peers = 2 * lax.axis_size("yl") * lax.axis_size("x")
    natom = atoms * lax.axis_size("yl") * lax.axis_size("x")
    frame_count = frames * 4 * chips
    ring = 2 * steps
    upward = [(i, (i + 1) % ring) for i in range(ring)]
    downward = [(i, (i - 1) % ring) for i in range(ring)]
    core = lax.axis_index("core").astype(jnp.int32).reshape(1)
    place = jnp.concatenate([lax.axis_index("zp").astype(jnp.int32).reshape(1), core])
    x_rows = frames_xyz.transpose(1, 0, 2).reshape(rows, atoms)
    vec_rows = vector_block.transpose(1, 0, 2).reshape(lanes, own_atoms)
    vmem, hbm = pl.BlockSpec(memory_space=pltpu.VMEM), pl.BlockSpec(memory_space=pl.ANY)
    limits = pltpu.CompilerParams(vmem_limit_bytes=16 * MIB)
    copies = pl.pallas_call(
        copies_kernel,
        in_specs=[hbm],
        out_specs=hbm,
        out_shape=jax.ShapeDtypeStruct((chips, lanes, own_atoms), BF16),
        scratch_shapes=[pltpu.SemaphoreType.DMA((chips,))],
        compiler_params=limits,
        cost_estimate=cost(1, 1),
        name="vector_copies",
    )(vec_rows)
    same = lax.all_to_all(copies, ("yh", "zh"), 0, 0, tiled=True)
    wide, narrow = atoms // steps, atoms // steps // 4
    both = lambda height: pl.BlockSpec((2, height, narrow), lambda step: (0, 0, step))
    part = lambda height, which: pl.BlockSpec((1, height, narrow), lambda step: (which, 0, step))
    sorted_shape = lambda height: jax.ShapeDtypeStruct((2, height, steps * narrow), BF16)
    keep, send, side, cross = pl.pallas_call(
        cross_kernel,
        grid=(steps,),
        in_specs=[
            SMEM_SPEC,
            pl.BlockSpec((rows, wide), lambda step: (0, step)),
            pl.BlockSpec((3, wide), lambda step: (0, step)),
        ],
        out_specs=[both(rows), both(rows), both(EXTRA), whole(peers, 8, rows + EXTRA)],
        out_shape=[
            sorted_shape(rows), sorted_shape(rows), sorted_shape(EXTRA), jax.ShapeDtypeStruct((peers, 8, rows + EXTRA), F32),
        ],
        scratch_shapes=[pltpu.VMEM((rows + EXTRA, EXTRA), F32)],
        compiler_params=params(),
        cost_estimate=cost(2 * rows * atoms * 256, 4 * rows * atoms),
        name="cross_terms",
    )(place, x_rows, mean_xyz)
    recv = lax.ppermute(send, "core", [(0, 1), (1, 0)])
    core_after = pl.pallas_call(
        pass_kernel,
        in_specs=[SMEM_SPEC, hbm],
        out_specs=SMEM_SPEC,
        out_shape=jax.ShapeDtypeStruct((1,), jnp.int32),
        cost_estimate=cost(PASS_FLOPS, 10**6),
        name="pass_core",
    )(core, cross)
    cross, core_after, same = lax.optimization_barrier((cross, core_after, same))
    opposite = lax.ppermute(same, ("zh", "zp"), downward)
    parts = lax.all_to_all(cross, ("core", "yl", "x"), 0, 0, tiled=True)
    blocks = lambda count: pl.BlockSpec((count, lanes, LANES), lambda step: (step, 0, 0))
    gram_rows = 2 * rows + EXTRA
    chunks = 2 if steps > 1 else 1
    fetched = [pltpu.VMEM((1, rows, steps * narrow), BF16)] * 2 + [pltpu.SemaphoreType.DMA((2, chunks))]
    def products(other, vec, *before):
        return pl.pallas_call(
            functools.partial(gram_kernel, quads, other),
            in_specs=[hbm, hbm, vmem, vmem] + [vmem] * len(before),
            out_specs=vmem,
            out_shape=jax.ShapeDtypeStruct((gram_rows, lanes), F32),
            scratch_shapes=[
                *fetched,
            ],
            compiler_params=pltpu.CompilerParams(vmem_limit_bytes=GRAM_LIMIT * MIB),
            cost_estimate=cost(GRAM_FLOPS, 10**6),
            name="vector_products",
        )(keep, recv, side, vec, *before)

    gram = products(1, opposite, products(0, same))
    rot_shape = (8 * frames + 8, lanes)
    rot, proj = pl.pallas_call(
        functools.partial(rotation_kernel, natom),
        in_specs=[SMEM_SPEC, vmem, vmem],
        out_specs=[vmem, vmem],
        out_shape=[
            jax.ShapeDtypeStruct(rot_shape, F32),
            jax.ShapeDtypeStruct((peers, frames // 2, 4 * kcount), BF16),
        ],
        compiler_params=limits,
        cost_estimate=cost(ROTATION_FLOPS, 10**6),
        name="rotation_projection",
    )(core_after, parts, gram)
    proj_parts = lax.all_to_all(proj, ("core", "yl", "x"), 0, 0, tiled=True)
    ups = chips * UP_SHARE // 16
    up, down, weight = pl.pallas_call(
        functools.partial(product_kernel, 1.0 / frame_count, quads),
        in_specs=[SMEM_SPEC, vmem, vmem, hbm, hbm, vmem],
        out_specs=[vmem, vmem, vmem],
        out_shape=[
            jax.ShapeDtypeStruct((ups, lanes, own_atoms), BF16),
            jax.ShapeDtypeStruct((chips - ups, lanes, own_atoms), BF16),
            jax.ShapeDtypeStruct((3 * lanes, gram_rows), BF16),
        ],
        scratch_shapes=fetched,
        compiler_params=limits,
        cost_estimate=cost(1, 1),
        name="product_terms",
    )(core, proj_parts, rot, keep, recv, side)
    from_below = lax.ppermute(up, ("zh", "zp"), upward)
    from_above = lax.ppermute(down, ("zh", "zp"), downward)
    own = pl.pallas_call(
        product_same_kernel,
        in_specs=[vmem, hbm, hbm, vmem],
        out_specs=vmem,
        out_shape=jax.ShapeDtypeStruct((quads, steps, lanes, LANES), F32),
        scratch_shapes=fetched,
        compiler_params=limits,
        cost_estimate=cost(2 * rows * atoms * 256, 4 * rows * atoms),
        name="product_terms_same",
    )(weight, keep, recv, side)
    neighbours = jnp.concatenate([from_below, from_above], axis=0)
    term = (own.reshape(neighbours.shape) + neighbours.astype(F32)).astype(BF16)
    terms = lax.all_to_all(term, ("yh", "zh"), 0, 0, tiled=True)
    total = jnp.sum(terms.astype(F32), axis=0)
    return total.reshape(3, kcount, own_atoms).transpose(1, 0, 2)


def solution(mesh):
    inner = Mesh(mesh.devices.reshape(mesh_sizes(mesh)), ("zh", "zp", "yh", "core", "yl", "x"))
    frames, coords = ("zh", "zp", "yh", "core"), ("yl", "x")
    in_specs = (P(frames, None, coords), P(None, coords), P(None, None, coords + frames))
    out_specs = P(None, None, coords + frames)
    return jax.shard_map(body, mesh=inner, in_specs=in_specs, out_specs=out_specs, check_vma=False)


def mesh_sizes(mesh):
    frames, coords = mesh.shape["frames"], mesh.shape["coords"]
    return (frames // 16, 2, 4, 2, 2, coords // 2)
```

```python
import functools

import jax
import jax.numpy as jnp
from jax import lax
from jax.experimental import pallas as pl
from jax.experimental.pallas import tpu as pltpu
from jax.sharding import Mesh
from jax.sharding import PartitionSpec as P

NS_STEPS = 8
LANES = 128
PAIR = 256
EXTRA = 16
F32 = jnp.float32
BF16 = jnp.bfloat16
HIGHEST = lax.Precision.HIGHEST
NT = (((1,), (1,)), ((), ()))
TN = (((0,), (0,)), ((), ()))


def iota(shape, dim):
    return lax.broadcasted_iota(jnp.int32, shape, dim)


def split3(value):
    high = value.astype(BF16)
    rest = value - high.astype(F32)
    middle = rest.astype(BF16)
    low = (rest - middle.astype(F32)).astype(BF16)
    return high, middle, low


def mean_rows(mean):
    shape = (EXTRA, mean.shape[1])
    row = iota(shape, 0)
    spread = jnp.where(row == 9, 1.0, 0.0)
    for i in range(3):
        spread = jnp.where((row < 9) & (row % 3 == i), mean[i : i + 1, :], spread)
    high, middle, low = split3(spread)
    take = jnp.where((row >= 3) & (row < 6), middle.astype(F32), jnp.where((row >= 6) & (row < 9), low.astype(F32), high.astype(F32)))
    return take.astype(BF16)


def cross_kernel(place_ref, x_ref, mean_ref, keep_ref, send_ref, rows_ref, cross_ref, acc_ref):
    step = pl.program_id(0)
    parity, core = place_ref[0], place_ref[1]
    extra = mean_rows(mean_ref[...])
    width = x_ref.shape[1]

    @pl.when(step == 0)
    def _():
        acc_ref[...] = jnp.zeros_like(acc_ref)

    total = acc_ref[...]
    pairs = width // PAIR
    for pair in range(pairs):
        columns = slice(pair * PAIR, (pair + 1) * PAIR)
        side = extra[:, columns]
        left = jnp.concatenate([x_ref[:, columns], side], axis=0)
        total += lax.dot_general(left, side, NT, preferred_element_type=F32)
        block = slice(pair % (pairs // 2) * LANES, (pair % (pairs // 2) + 1) * LANES)
        first, second = left[:, :LANES], left[:, LANES:]
        mine = jnp.where(core == 0, first, second)
        theirs = jnp.where(core == 0, second, first)
        other = (parity + pair // (pairs // 2)) % 2
        keep_ref[other, :, block] = mine[:-EXTRA]
        send_ref[other, :, block] = theirs[:-EXTRA]
        rows_ref[other, :, block] = mine[-EXTRA:]
    acc_ref[...] = total

    @pl.when(step == pl.num_programs(0) - 1)
    def _():
        row, col = iota((8, EXTRA), 0), iota((8, EXTRA), 1)
        pick = ((row < 3) & (col < 9) & ((col == row) | (col == row + 3) | (col == row + 6))) | ((row == 3) & (col == 9))
        cross = lax.dot_general(pick.astype(F32), total, NT, precision=HIGHEST, preferred_element_type=F32)
        cross_ref[...] = jnp.broadcast_to(cross[None, :4], cross_ref.shape)


def polar_factor(amat):
    for _ in range(NS_STEPS):
        square = [[sum(amat[i][j] * amat[k][j] for j in range(3)) for k in range(3)] for i in range(3)]
        amat = [[1.5 * amat[i][j] - 0.5 * sum(square[i][k] * amat[k][j] for k in range(3)) for j in range(3)] for i in range(3)]
    return amat


def rotation_kernel(natom, core_ref, parts_ref, gram_ref, out_ref, proj_ref):
    half = parts_ref.shape[0] // 2
    frames = (parts_ref.shape[2] - EXTRA) // 3
    lanes = out_ref.shape[1]
    first, second = parts_ref[0], parts_ref[half]
    for index in range(1, half):
        first += parts_ref[index]
        second += parts_ref[half + index]
    is_first = core_ref[0] == 0
    own = jnp.where(is_first, first, second)
    other = jnp.where(is_first, second, first)
    ones_at = 3 * frames + 9
    centre = [own[i : i + 1, ones_at : ones_at + 1] / natom for i in range(3)]
    columns = [[total[:, j * frames : (j + 1) * frames] for total in (own, other)] for j in range(3)]
    row = lambda index, j: jnp.concatenate([part[index : index + 1] for part in columns[j]], axis=0)
    sums = [row(3, j) for j in range(3)]
    cross = [[row(i, j) - centre[i] * sums[j] for j in range(3)] for i in range(3)]
    scale = jnp.sqrt(1.0 + sum(cross[i][j] * cross[i][j] for i in range(3) for j in range(3)))
    rotation = polar_factor([[cross[i][j] / scale for j in range(3)] for i in range(3)])
    shift = [sum(rotation[i][j] * (sums[j] / natom) for j in range(3)) for i in range(3)]
    entries = [rotation[i][j] for i in range(3) for j in range(3)] + shift
    at = iota((EXTRA, frames), 0)
    index3, lane = iota((3 * EXTRA, 4 * LANES), 0) % EXTRA, iota((3 * EXTRA, 4 * LANES), 1)
    third = lanes // 3
    place, within = lane // LANES, lane % LANES
    which = within // third
    chosen = ((place < 3) & (index3 == 3 * which + place)) | ((place == 3) & (index3 == 9 + which))
    chosen = jnp.where(chosen & (which < 3), 1.0, 0.0).astype(BF16)
    for side in range(2):
        packed = jnp.zeros((EXTRA, frames), F32)
        for index, entry in enumerate(entries):
            packed = jnp.where(at == index, entry[side : side + 1], packed)
        pieces = jnp.concatenate([piece.astype(F32) for piece in split3(packed)], axis=0).astype(BF16)
        spread = lax.dot_general(pieces, chosen, TN, preferred_element_type=F32)
        for index in range(4):
            begin = (2 * index + side) * frames
            out_ref[begin : begin + frames, :] = spread[:, index * LANES : index * LANES + lanes]
    which8 = lane_part((8, lanes))
    out_ref[8 * frames : 8 * frames + 8, :] = jnp.where(which8 == 0, centre[0], jnp.where(which8 == 1, centre[1], centre[2]))
    proj = packed_projection(is_first, gram_ref, out_ref, frames)
    proj_ref[...] = jnp.broadcast_to(proj.astype(BF16)[None], proj_ref.shape)


def lane_part(shape):
    lane = iota(shape, 1)
    third = shape[1] // 3
    return (lane >= third).astype(jnp.int32) + (lane >= 2 * third).astype(jnp.int32)


def fetch(refs, buffers, sems, others, chunks):
    width = refs[0].shape[2] // chunks
    copies = []
    for index, other in enumerate(others):
        for chunk in range(chunks):
            columns = pl.ds(chunk * width, width)
            group = []
            for which, (ref, buffer) in enumerate(zip(refs, buffers)):
                copy = pltpu.make_async_copy(
                    ref.at[other, :, columns], buffer.at[index, :, columns], sems.at[which, index * chunks + chunk]
                )
                copy.start()
                group.append(copy)
            copies.append(group)
    return copies


def copies_kernel(vec_ref, out_ref, sems):
    copies = [pltpu.make_async_copy(vec_ref, out_ref.at[index], sems.at[index]) for index in range(out_ref.shape[0])]
    for copy in copies:
        copy.start()
    for copy in copies:
        copy.wait()


def pass_kernel(core_ref, after_ref, out_ref):
    out_ref[0] = core_ref[0]


def by_yh(at, quads, pairs):
    return at % quads * (2 * pairs // quads) + at // quads


def gram_kernel(quads, other, keep_hbm, recv_hbm, rows_ref, vec_ref, *rest):
    before, (out_ref, keep_ref, recv_ref, sems) = rest[:-4], rest[-4:]
    copies = fetch((keep_hbm, recv_hbm), (keep_ref, recv_ref), sems, (other,), sems.shape[1])
    total = before[0][...] if before else jnp.zeros(out_ref.shape, F32)
    chunks, pairs = len(copies), vec_ref.shape[0] // 2
    for pair in range(pairs):
        if pair % (pairs // chunks) == 0:
            for copy in copies[pair // (pairs // chunks)]:
                copy.wait()
        columns = slice(pair * PAIR, (pair + 1) * PAIR)
        left = jnp.concatenate([keep_ref[0, :, columns], recv_ref[0, :, columns], rows_ref[other, :, columns]], axis=0)
        right = jnp.concatenate([vec_ref[by_yh(at, quads, pairs)] for at in (2 * pair, 2 * pair + 1)], axis=1)
        total += lax.dot_general(left, right, NT, preferred_element_type=F32)
    out_ref[...] = total


def packed_projection(is_first, gram_ref, rot_ref, frames):
    lanes = gram_ref.shape[1]
    third = lanes // 3
    extra = gram_ref[6 * frames :, :]
    vec_sums = extra[9:10, :]
    centre = rot_ref[8 * frames : 8 * frames + 1, :]
    part = lane_part((1, lanes))
    along = [extra[i : i + 1] + extra[3 + i : 4 + i] + extra[6 + i : 7 + i] for i in range(3)]
    mean_term = jnp.where(part == 0, along[0], jnp.where(part == 1, along[1], along[2])) - centre * vec_sums
    halves = []
    for side in range(2):
        value = -rot_ref[(6 + side) * frames : (7 + side) * frames, :] * vec_sums - mean_term
        for j in range(3):
            spread = rot_ref[(2 * j + side) * frames : (2 * j + side + 1) * frames, :]
            begin = (3 * side + j) * frames
            value += spread * gram_ref[begin : begin + frames, :]
        halves.append(value)
    first = jnp.where(is_first, halves[0], halves[1])
    second = jnp.where(is_first, halves[1], halves[0])
    value = jnp.concatenate([first, second], axis=0)
    quarter = frames // 2
    row, col = iota((lanes, 4 * third), 0), iota((lanes, 4 * third), 1)
    packed = jnp.zeros((quarter, 4 * third), F32)
    pieces = split3(value)
    for q in range(4):
        fold = jnp.where((row % third == col % third) & (col // third == q), 1.0, 0.0).astype(BF16)
        for piece in pieces:
            packed += jnp.dot(piece[q * quarter : (q + 1) * quarter, :], fold, preferred_element_type=F32)
    return packed


def product_weights(is_first, parts_ref, rot_ref, weight_ref, frames, scale):
    lanes = rot_ref.shape[1]
    third = lanes // 3

    packed = parts_ref[0].astype(F32)
    for index in range(1, parts_ref.shape[0]):
        packed += parts_ref[index].astype(F32)
    packed = packed.astype(BF16)
    row, col = iota((4 * third, lanes), 0), iota((4 * third, lanes), 1)
    quarters = []
    for q in range(4):
        unfold = (row % third == col % third) & (row // third == q)
        quarters.append(jnp.dot(packed, unfold.astype(F32).astype(BF16), preferred_element_type=F32))
    first = jnp.concatenate(quarters[:2], axis=0)
    second = jnp.concatenate(quarters[2:], axis=0)
    sides = (jnp.where(is_first, first, second), jnp.where(is_first, second, first))
    centre = rot_ref[8 * frames : 8 * frames + 1, :]
    pieces = []
    proj_sum = jnp.zeros((1, lanes), F32)
    shift_sum = jnp.zeros((1, lanes), F32)
    for side in range(2):
        for j in range(3):
            begin = (2 * j + side) * frames
            pieces.append(rot_ref[begin : begin + frames, :] * sides[side])
        proj_sum += jnp.sum(sides[side], axis=0, keepdims=True)
        shift = rot_ref[(6 + side) * frames : (7 + side) * frames, :]
        shift_sum += jnp.sum(sides[side] * shift, axis=0, keepdims=True)
    at, part = iota((EXTRA, lanes), 0), lane_part((EXTRA, lanes))
    is_mean = (at < 9) & ((at == part) | (at == part + 3) | (at == part + 6))
    tail = jnp.where(is_mean, -proj_sum, jnp.where(at == 9, centre * proj_sum - shift_sum, 0.0))
    weight = jnp.concatenate(pieces + [tail], axis=0) * scale
    same = (iota((lanes, lanes), 0) == iota((lanes, lanes), 1)).astype(F32).astype(BF16)
    for index, piece in enumerate(split3(weight)):
        turned = lax.dot_general(same, piece, NT, preferred_element_type=F32)
        weight_ref[index * lanes : (index + 1) * lanes, :] = turned.astype(BF16)


def weighted(weight, refs, columns):
    term = jnp.dot(weight, jnp.concatenate([ref[0, :, columns] for ref in refs], axis=0), preferred_element_type=F32)
    lanes = term.shape[0] // 3
    return term[2 * lanes :] + term[lanes : 2 * lanes] + term[:lanes]


def product_kernel(
    scale, quads, core_ref, parts_ref, rot_ref, keep_hbm, recv_hbm, rows_ref, up_ref, down_ref, weight_ref, keep_ref, recv_ref, sems
):
    chunks = sems.shape[1]
    copies = fetch((keep_hbm, recv_hbm), (keep_ref, recv_ref), sems, (1,), chunks)
    product_weights(core_ref[0] == 0, parts_ref, rot_ref, weight_ref, keep_ref.shape[1] // 3, scale)
    weight = weight_ref[...]
    pairs = (up_ref.shape[0] + down_ref.shape[0]) // 2
    for pair in range(pairs):
        if pair % (pairs // chunks) == 0:
            for copy in copies[pair // (pairs // chunks)]:
                copy.wait()
        columns = slice(pair * PAIR, (pair + 1) * PAIR)
        term = weighted(weight, (keep_ref, recv_ref, rows_ref.at[pl.ds(1, 1)]), columns).astype(BF16)
        for index in range(2):
            at = by_yh(2 * pair + index, quads, pairs)
            ref, at = (up_ref, at) if at < up_ref.shape[0] else (down_ref, at - up_ref.shape[0])
            ref[at] = term[:, index * LANES : (index + 1) * LANES]


def product_same_kernel(weight_ref, keep_hbm, recv_hbm, rows_ref, out_ref, keep_ref, recv_ref, sems):
    chunks = sems.shape[1]
    copies = fetch((keep_hbm, recv_hbm), (keep_ref, recv_ref), sems, (0,), chunks)
    weight = weight_ref[...]
    quads = out_ref.shape[0]
    pairs = quads * out_ref.shape[1] // 2
    for pair in range(pairs):
        if pair % (pairs // chunks) == 0:
            for copy in copies[pair // (pairs // chunks)]:
                copy.wait()
        columns = slice(pair * PAIR, (pair + 1) * PAIR)
        term = weighted(weight, (keep_ref, recv_ref, rows_ref.at[pl.ds(0, 1)]), columns)
        for index in range(2):
            high, quad = divmod(2 * pair + index, quads)
            out_ref[quad, high] = term[:, index * LANES : (index + 1) * LANES]


MIB = 1024 * 1024
UP_SHARE = 10
GRAM_LIMIT = 16
GRAM_FLOPS = 1
ROTATION_FLOPS = 10**9
PASS_FLOPS = 40000000000
SMEM_SPEC = pl.BlockSpec(memory_space=pltpu.SMEM)


def params(limit=16):
    return pltpu.CompilerParams(vmem_limit_bytes=limit * MIB, dimension_semantics=("arbitrary",))


def cost(flops, moved):
    return pl.CostEstimate(flops=flops, bytes_accessed=moved, transcendentals=0)


def whole(*shape):
    return pl.BlockSpec(shape, lambda step: (0,) * len(shape))


def body(frames_xyz, mean_xyz, vector_block):
    frames, _, atoms = frames_xyz.shape
    kcount, _, own_atoms = vector_block.shape
    lanes = 3 * kcount
    rows = 3 * frames
    steps, quads = lax.axis_size("zh"), lax.axis_size("yh")
    chips = steps * quads
    peers = 2 * lax.axis_size("yl") * lax.axis_size("x")
    natom = atoms * lax.axis_size("yl") * lax.axis_size("x")
    frame_count = frames * 4 * chips
    ring = 2 * steps
    upward = [(i, (i + 1) % ring) for i in range(ring)]
    downward = [(i, (i - 1) % ring) for i in range(ring)]
    core = lax.axis_index("core").astype(jnp.int32).reshape(1)
    place = jnp.concatenate([lax.axis_index("zp").astype(jnp.int32).reshape(1), core])
    x_rows = frames_xyz.transpose(1, 0, 2).reshape(rows, atoms)
    vec_rows = vector_block.transpose(1, 0, 2).reshape(lanes, own_atoms)
    vmem, hbm = pl.BlockSpec(memory_space=pltpu.VMEM), pl.BlockSpec(memory_space=pl.ANY)
    limits = pltpu.CompilerParams(vmem_limit_bytes=16 * MIB)
    copies = pl.pallas_call(
        copies_kernel,
        in_specs=[hbm],
        out_specs=hbm,
        out_shape=jax.ShapeDtypeStruct((chips, lanes, own_atoms), BF16),
        scratch_shapes=[pltpu.SemaphoreType.DMA((chips,))],
        compiler_params=limits,
        cost_estimate=cost(1, 1),
        name="vector_copies",
    )(vec_rows)
    same = lax.all_to_all(copies, ("yh", "zh"), 0, 0, tiled=True)
    wide, narrow = atoms // steps, atoms // steps // 4
    both = lambda height: pl.BlockSpec((2, height, narrow), lambda step: (0, 0, step))
    part = lambda height, which: pl.BlockSpec((1, height, narrow), lambda step: (which, 0, step))
    sorted_shape = lambda height: jax.ShapeDtypeStruct((2, height, steps * narrow), BF16)
    keep, send, side, cross = pl.pallas_call(
        cross_kernel,
        grid=(steps,),
        in_specs=[
            SMEM_SPEC,
            pl.BlockSpec((rows, wide), lambda step: (0, step)),
            pl.BlockSpec((3, wide), lambda step: (0, step)),
        ],
        out_specs=[both(rows), both(rows), both(EXTRA), whole(peers, 4, rows + EXTRA)],
        out_shape=[
            sorted_shape(rows), sorted_shape(rows), sorted_shape(EXTRA), jax.ShapeDtypeStruct((peers, 4, rows + EXTRA), F32),
        ],
        scratch_shapes=[pltpu.VMEM((rows + EXTRA, EXTRA), F32)],
        compiler_params=params(),
        cost_estimate=cost(2 * rows * atoms * 256, 4 * rows * atoms),
        name="cross_terms",
    )(place, x_rows, mean_xyz)
    recv = lax.ppermute(send, "core", [(0, 1), (1, 0)])
    core_after = pl.pallas_call(
        pass_kernel,
        in_specs=[SMEM_SPEC, hbm],
        out_specs=SMEM_SPEC,
        out_shape=jax.ShapeDtypeStruct((1,), jnp.int32),
        cost_estimate=cost(PASS_FLOPS, 10**6),
        name="pass_core",
    )(core, cross)
    cross, core_after, same = lax.optimization_barrier((cross, core_after, same))
    opposite = lax.ppermute(same, ("zh", "zp"), downward)
    parts = lax.all_to_all(cross, ("core", "yl", "x"), 0, 0, tiled=True)
    blocks = lambda count: pl.BlockSpec((count, lanes, LANES), lambda step: (step, 0, 0))
    gram_rows = 2 * rows + EXTRA
    chunks = 2 if steps > 1 else 1
    fetched = [pltpu.VMEM((1, rows, steps * narrow), BF16)] * 2 + [pltpu.SemaphoreType.DMA((2, chunks))]
    def products(other, vec, *before):
        return pl.pallas_call(
            functools.partial(gram_kernel, quads, other),
            in_specs=[hbm, hbm, vmem, vmem] + [vmem] * len(before),
            out_specs=vmem,
            out_shape=jax.ShapeDtypeStruct((gram_rows, lanes), F32),
            scratch_shapes=[
                *fetched,
            ],
            compiler_params=pltpu.CompilerParams(vmem_limit_bytes=GRAM_LIMIT * MIB),
            cost_estimate=cost(GRAM_FLOPS, 10**6),
            name="vector_products",
        )(keep, recv, side, vec, *before)

    gram = products(1, opposite, products(0, same))
    rot_shape = (8 * frames + 8, lanes)
    rot, proj = pl.pallas_call(
        functools.partial(rotation_kernel, natom),
        in_specs=[SMEM_SPEC, vmem, vmem],
        out_specs=[vmem, vmem],
        out_shape=[
            jax.ShapeDtypeStruct(rot_shape, F32),
            jax.ShapeDtypeStruct((peers, frames // 2, 4 * kcount), BF16),
        ],
        compiler_params=limits,
        cost_estimate=cost(ROTATION_FLOPS, 10**6),
        name="rotation_projection",
    )(core_after, parts, gram)
    proj_parts = lax.all_to_all(proj, ("core", "yl", "x"), 0, 0, tiled=True)
    ups = chips * UP_SHARE // 16
    up, down, weight = pl.pallas_call(
        functools.partial(product_kernel, 1.0 / frame_count, quads),
        in_specs=[SMEM_SPEC, vmem, vmem, hbm, hbm, vmem],
        out_specs=[vmem, vmem, vmem],
        out_shape=[
            jax.ShapeDtypeStruct((ups, lanes, own_atoms), BF16),
            jax.ShapeDtypeStruct((chips - ups, lanes, own_atoms), BF16),
            jax.ShapeDtypeStruct((3 * lanes, gram_rows), BF16),
        ],
        scratch_shapes=fetched,
        compiler_params=limits,
        cost_estimate=cost(1, 1),
        name="product_terms",
    )(core, proj_parts, rot, keep, recv, side)
    from_below = lax.ppermute(up, ("zh", "zp"), upward)
    from_above = lax.ppermute(down, ("zh", "zp"), downward)
    own = pl.pallas_call(
        product_same_kernel,
        in_specs=[vmem, hbm, hbm, vmem],
        out_specs=vmem,
        out_shape=jax.ShapeDtypeStruct((quads, steps, lanes, LANES), F32),
        scratch_shapes=fetched,
        compiler_params=limits,
        cost_estimate=cost(2 * rows * atoms * 256, 4 * rows * atoms),
        name="product_terms_same",
    )(weight, keep, recv, side)
    neighbours = jnp.concatenate([from_below, from_above], axis=0)
    term = (own.reshape(neighbours.shape) + neighbours.astype(F32)).astype(BF16)
    terms = lax.all_to_all(term, ("yh", "zh"), 0, 0, tiled=True)
    total = jnp.sum(terms.astype(F32), axis=0)
    return total.reshape(3, kcount, own_atoms).transpose(1, 0, 2)


def solution(mesh):
    inner = Mesh(mesh.devices.reshape(mesh_sizes(mesh)), ("zh", "zp", "yh", "core", "yl", "x"))
    frames, coords = ("zh", "zp", "yh", "core"), ("yl", "x")
    in_specs = (P(frames, None, coords), P(None, coords), P(None, None, coords + frames))
    out_specs = P(None, None, coords + frames)
    return jax.shard_map(body, mesh=inner, in_specs=in_specs, out_specs=out_specs, check_vma=False)


def mesh_sizes(mesh):
    frames, coords = mesh.shape["frames"], mesh.shape["coords"]
    return (frames // 16, 2, 4, 2, 2, coords // 2)
```
